32 devices in a mesh: dp: 16 (over z, y, core), tensor: 2 (over x).
Axes of the slice: x: 2, y: 2, z: 4, core: 2. Of those that a mesh axis runs over, the one named last changes fastest.
Arguments:
- tokens: bfloat16 [1024, 8192], P(('dp', 'tensor')), may hold values from -6 to 6
- gain: float32 [8192], replicated, may hold values from 0.1 to 1.9
- stale: bfloat16 [8192, 2048], P(None, 'tensor'), may hold values from -0.0625 to 0.0625
- bias: float32 [2048], P('tensor'), may hold values from -3 to 3
- first: float32 [8192, 2048], P(('dp', 'tensor')), may hold values from -6 to 6
- second: float32 [8192, 2048], P(('dp', 'tensor')), may hold values from 0.1 to 10
- grad: float32 [8192, 2048], P(('dp', 'tensor')), may hold values from -6 to 6
- residual: float32 [8192, 2048], P(('dp', 'tensor')), may hold values from -0.12 to 0.12
- exponent: int32 [256, 16], P(('dp', 'tensor')), may hold values from 10 to 17
Outputs:
- new_first: float32 [8192, 2048], P(('dp', 'tensor'))
- new_second: float32 [8192, 2048], P(('dp', 'tensor'))
- projected: bfloat16 [1024, 2048], P('dp', 'tensor')
The draws below stay inside these ranges and needn't reach their ends.
All inputs are finite; a program needn't handle non-finite values.
Results may differ from the reference program's by a relative error of at most 0.0062.
Values may be sent and summed in bfloat16 or wider, within the bound.
No kernel may reach another device: no remote copies, remote signals or barrier semaphores. Data moves between devices by JAX's collectives and lax.ppermute only.
A program may use at most 128 MiB of HBM per device.

```python
import math
import jax
import jax.numpy as jnp
from jax import lax

D = 8192
QROWS = 32
QCOL = 128
WIDE = 2048
TOKENS = 1024


def plant(drawn, own_key, smallest, largest):
    place = [jax.random.randint(jax.random.fold_in(own_key, axis), (), 0, length) for axis, length in enumerate(drawn.shape)]
    longest = drawn.shape.index(max(drawn.shape))
    next_to = place[:longest] + [(place[longest] + 1) % drawn.shape[longest]] + place[longest + 1:]
    return drawn.at[tuple(place)].set(smallest).at[tuple(next_to)].set(largest)


def level_of(stream_key, dims, split, smallest, largest):
    factor_of = 1.0
    for dim, parts in split:
        draws = jax.random.uniform(jax.random.fold_in(jax.random.fold_in(stream_key, 6), dim), (parts,), jnp.float32, smallest / len(split), largest / len(split))
        factor_of = factor_of * jnp.repeat(jnp.exp(draws), dims[dim] // parts).reshape((-1,) + (1,) * (len(dims) - 1 - dim))
    return factor_of


def gaussian(rng, extent, scale, most, split=(), kind=jnp.bfloat16):
    entries = jax.random.normal(rng, extent, jnp.float32) * scale
    if len(split) > 0:
        entries = level_of(rng, extent, split, -0.22, 0.18) * entries
    return jnp.clip(entries, min=-most, max=most).astype(kind)


def setup_inputs(seed: int = 0) -> dict:
    key_list = jax.random.split(jax.random.key(seed), 10)
    return {
        "tokens": gaussian(key_list[0], (TOKENS, D), 1.0, 6.0, ((0, 32),)),
        "gain": jnp.clip(1.0 + 0.18 * jax.random.normal(key_list[1], (D,), jnp.float32), 0.1, 1.9),
        "stale": gaussian(key_list[2], (D, WIDE), D ** -0.5, 0.0625, ((1, 2),)),
        "bias": gaussian(key_list[3], (WIDE,), 0.5, 3.0, ((0, 2),), jnp.float32),
        "first": gaussian(key_list[4], (D, WIDE), 1.0, 6.0, ((0, 32),), jnp.float32),
        "second": jnp.clip(jnp.exp(math.log(10.0) - 4.6051702 * jax.random.uniform(key_list[5], (D, WIDE), jnp.float32) ** level_of(key_list[5], (D, WIDE), ((0, 32),), -0.2, 0.2)), 0.1, 10.0),
        "grad": gaussian(key_list[6], (D, WIDE), 1.0, 6.0, ((0, 32),), jnp.float32),
        "residual": gaussian(key_list[7], (D, WIDE), 0.02, 0.12, ((0, 32),), jnp.float32),
        "exponent": plant(jax.random.randint(key_list[8], (D // QROWS, WIDE // QCOL), 10, 18), jax.random.fold_in(key_list[8], 1), 10, 17).astype(jnp.int32),
    }


def reference(tokens, gain, stale, bias, first, second, grad, residual, exponent):
    new_first = 0.9 * first + 0.1 * grad
    new_second = 0.95 * second + 0.05 * grad * grad
    corrected = 0.02 * new_first / (jnp.sqrt(new_second) + 1e-08) + residual
    expo = exponent.astype(jnp.float32)
    upward = jnp.exp2(expo)[:, None, :, None]
    downward = jnp.exp2(-expo)[:, None, :, None]
    blocks_rows = exponent.shape[0]
    blocks_cols = exponent.shape[1]
    blocked = corrected.reshape(blocks_rows, QROWS, blocks_cols, QCOL) * upward
    quant = jnp.clip(blocked, -448.0, 448.0).astype(jnp.bfloat16)
    quant = lax.optimization_barrier(quant)
    delta = (quant.astype(jnp.float32) * downward).reshape(D, WIDE).astype(jnp.bfloat16)
    weight = (stale.astype(jnp.float32) + delta.astype(jnp.float32)).astype(jnp.bfloat16)
    values = tokens.astype(jnp.float32)
    meansq = lax.optimization_barrier(jnp.mean(values * values, axis=1, keepdims=True))
    normed = (values * lax.rsqrt(meansq + 1e-06) * gain[None, :]).astype(jnp.bfloat16)
    product = jnp.dot(normed, weight, preferred_element_type=jnp.float32)
    projected = (product + bias[None, :]).astype(jnp.bfloat16)
    return (new_first, new_second, projected)
```

```python
import functools

import jax
import jax.numpy as jnp
from jax import lax
from jax.experimental import pallas as pl
from jax.experimental.pallas import tpu as pltpu
from jax.sharding import PartitionSpec as P

PAIR = 2
CLIP = 448.0
LIMIT = 28 * 1024 * 1024
F32 = jnp.float32
BF16 = jnp.bfloat16
FAR = pl.BlockSpec(memory_space=pltpu.HBM)
NEAR = pl.BlockSpec(memory_space=pltpu.VMEM)


def far(x):
    return pltpu.with_memory_space_constraint(x, pltpu.HBM)


def like(shape, dtype):
    return jax.ShapeDtypeStruct(shape, dtype)


def normalise(tokens_ref, gain_ref, piece_refs):
    slab = lax.axis_index("dp") // PAIR
    values = tokens_ref[...].astype(F32)
    scale = lax.rsqrt(jnp.mean(values * values, axis=1, keepdims=True) + 1e-06)
    width = piece_refs[0].shape[1]
    for k, piece_ref in enumerate(piece_refs):
        columns = pl.ds(pl.multiple_of((slab ^ k) * width, width), width)
        piece_ref[...] = (tokens_ref[:, columns].astype(F32) * scale * gain_ref[:, columns]).astype(BF16)


def adam_kernel(slabs, chunks, qrows, qcol, heads, start, count, *refs):
    expo_far, *inputs = refs[:5]
    extra = refs[5 : 5 + 2]
    n_in = 7
    new_first_out, new_second_out, delta_out = refs[n_in : n_in + 3]
    pieces = refs[n_in + 3 : n_in + 3 + slabs]
    b0, b1, b2, b3, n1, n2, expo_ref, sems, expo_sem, *rest = refs[n_in + 3 + slabs :]
    bufs = (b0, b1, b2, b3)
    mine = lax.axis_index("tensor")
    rows = inputs[0].shape[0]
    cols = inputs[0].shape[1] // heads
    groups = cols // qcol
    high = rows // chunks

    if slabs:
        tokens_ref, gain_ref, token_sem = rest
        loads = [
            pltpu.make_async_copy(extra[0], tokens_ref, token_sem.at[0]),
            pltpu.make_async_copy(extra[1], gain_ref, token_sem.at[1]),
        ]
        for load in loads:
            load.start()
    fetch_expo = pltpu.make_async_copy(expo_far, expo_ref, expo_sem)
    fetch_expo.start()

    def window(j, c):
        head = mine ^ (start + j)
        return pl.ds(c * high, high), pl.ds(pl.multiple_of(head * cols, cols), cols)

    steps = [(j, c) for j in range(count) for c in range(chunks)]
    fetches, stores = [], []
    for n, (j, c) in enumerate(steps):
        at = window(j, c)
        here = (j, pl.ds(c * high, high), slice(None))
        fetches.append([pltpu.make_async_copy(inputs[a].at[at], bufs[a].at[here], sems.at[n, a]) for a in range(4)])
        for f in fetches[-1]:
            f.start()
    if slabs:
        for load in loads:
            load.wait()
        normalise(tokens_ref, gain_ref, pieces)
    fetch_expo.wait()
    for n, (j, c) in enumerate(steps):
        head = mine ^ (start + j)
        for f in fetches[n]:
            f.wait()
        for b in range(high // qrows):
            row = c * (high // qrows) + b
            here = pl.ds(row * qrows, qrows)
            for g in range(groups):
                lanes = pl.ds(g * qcol, qcol)
                grad = b2[j, here, lanes]
                new_first = 0.9 * b0[j, here, lanes] + 0.1 * grad
                new_second = 0.95 * b1[j, here, lanes] + 0.05 * grad * grad
                n1[j, here, lanes] = new_first
                n2[j, here, lanes] = new_second
                bottom = new_second * lax.rsqrt(new_second) + 1e-08
                inverse = pl.reciprocal(bottom, approx=True)
                inverse = inverse * (2.0 - bottom * inverse)
                corrected = 0.02 * new_first * inverse + b3[j, here, lanes]
                expo = jnp.full((1, qcol), expo_ref[row, head * groups + g], jnp.int32).astype(F32)
                most = CLIP * jnp.exp2(-expo)
                delta_out[j, here, lanes] = jnp.clip(corrected, -most, most).astype(BF16)
        at = window(j, c)
        here = (j, pl.ds(c * high, high), slice(None))
        stores += [
            pltpu.make_async_copy(n1.at[here], new_first_out.at[at], sems.at[n, 4]),
            pltpu.make_async_copy(n2.at[here], new_second_out.at[at], sems.at[n, 5]),
        ]
        for s in stores[-2:]:
            s.start()
    for s in stores:
        s.wait()


def adam(arrays, exponent, heads, start, count, made=(), tokens=None, gain=None, slabs=0, chunks=2):
    rows, full = arrays[0].shape
    qrows, qcol = rows // exponent.shape[0], full // exponent.shape[1]
    cols = full // heads
    chunks = min(chunks, rows // qrows)
    held = pltpu.VMEM((count, rows, cols), F32)
    extra = tuple(made)
    scratch = [held] * 6 + [
        pltpu.SMEM(exponent.shape, jnp.int32),
        pltpu.SemaphoreType.DMA((count * chunks, 6)),
        pltpu.SemaphoreType.DMA(()),
    ]
    pieces = []
    if slabs:
        extra = (tokens, gain.reshape(1, -1))
        height, features = tokens.shape
        pieces = [like((height, features // slabs), BF16)] * slabs
        scratch += [pltpu.VMEM((height, features), BF16), pltpu.VMEM((1, features), F32), pltpu.SemaphoreType.DMA((2,))]
    size = 4 * rows * cols * count
    return pl.pallas_call(
        functools.partial(adam_kernel, slabs, chunks, qrows, qcol, heads, start, count),
        in_specs=[FAR] * (5 + len(extra)),
        out_specs=[FAR] * 2 + [NEAR] * (1 + slabs),
        out_shape=[like((rows, full), F32)] * 2 + [like((count, rows, cols), BF16)] + pieces,
        scratch_shapes=scratch,
        input_output_aliases={5: 0, 6: 1} if made else {},
        compiler_params=pltpu.CompilerParams(vmem_limit_bytes=LIMIT),
        cost_estimate=pl.CostEstimate(flops=0, bytes_accessed=0, transcendentals=0),
    )(*[far(x) for x in (exponent, *arrays, *extra)])


def place_rows(refs, heads, rows):
    core, mine = lax.axis_index("dp") % PAIR, lax.axis_index("tensor")
    for n, ref in enumerate(refs):
        at = ((core ^ (n // heads)) * heads + (mine ^ (n % heads))) * rows
        yield ref, pl.ds(pl.multiple_of(at, rows), rows)


def multiply(piece_refs, weight, out_refs):
    rows = piece_refs[0].shape[0]
    stacked = jnp.concatenate([r[...] for r in piece_refs], axis=0)
    total = jnp.dot(stacked, weight, preferred_element_type=F32)
    for k, out_ref in enumerate(out_refs):
        out_ref[...] = total[k * rows : (k + 1) * rows].astype(out_ref.dtype)


def merge_kernel(slabs, heads, stale_ref, *refs):
    delta_refs, piece_refs = refs[: PAIR * heads], refs[PAIR * heads : PAIR * heads + slabs]
    weight_ref, out_refs = refs[PAIR * heads + slabs], refs[PAIR * heads + slabs + 1 :]
    for ref, here in place_rows(delta_refs, heads, delta_refs[0].shape[0]):
        weight_ref[here, :] = (stale_ref[here, :].astype(F32) + ref[...].astype(F32)).astype(BF16)
    multiply(piece_refs, weight_ref[...], out_refs)


def product_kernel(slabs, *refs):
    multiply(refs[:slabs], refs[slabs][...], refs[slabs + 1 :])


def results_of(pieces, cols, own):
    shape = (pieces[0].shape[0], cols)
    return [like(shape, F32 if own and k == 0 else BF16) for k in range(len(pieces))]


def cost_of(pieces, depth, cols):
    rows = len(pieces) * pieces[0].shape[0]
    return pl.CostEstimate(flops=0, bytes_accessed=0, transcendentals=0)


def merge_product(stale, deltas, pieces, heads):
    depth, cols = stale.shape
    return pl.pallas_call(
        functools.partial(merge_kernel, len(pieces), heads),
        out_shape=[like((depth, cols), BF16)] + results_of(pieces, cols, True),
        compiler_params=pltpu.CompilerParams(vmem_limit_bytes=LIMIT),
        cost_estimate=cost_of(pieces, depth, cols),
    )(stale, *deltas, *pieces)


def product(pieces, weight, own):
    return pl.pallas_call(
        functools.partial(product_kernel, len(pieces)),
        out_shape=results_of(pieces, weight.shape[1], own),
        compiler_params=pltpu.CompilerParams(vmem_limit_bytes=LIMIT),
        cost_estimate=cost_of(pieces, *weight.shape),
    )(*pieces, weight)


def on_device(tokens, gain, stale, bias, first, second, grad, residual, exponent):
    heads = lax.axis_size("tensor")
    replicas = lax.axis_size("dp")
    slabs = replicas // PAIR
    slab, mine = lax.axis_index("dp") // PAIR, lax.axis_index("tensor")
    height = tokens.shape[0]

    def over_tensor(x, j):
        return x if j == 0 else lax.ppermute(x, "tensor", [(i, i ^ j) for i in range(heads)])

    def over_core(x, c):
        return x if c == 0 else lax.ppermute(x, "dp", [(i, i ^ c) for i in range(replicas)])

    def over_slab(x, k):
        return x if k == 0 else lax.ppermute(x, "dp", [(i, i ^ (k * PAIR)) for i in range(replicas)])

    arrays = (first, second, grad, residual)
    *made, theirs, normed = (lambda r: (r[0], r[1], r[2], r[3:]))(
        adam(arrays, exponent, heads, 1, heads - 1, tokens=tokens, gain=gain, slabs=slabs)
    )
    arrived = [over_tensor(theirs[j], j + 1) for j in range(heads - 1)]
    pieces = [None] * slabs
    for k in reversed(range(slabs)):
        pieces[k] = over_slab(normed[k], k)
    new_first, new_second, ours = adam(arrays, exponent, heads, 0, 1, made=made)
    ours, *pieces = lax.optimization_barrier((ours, *pieces))
    owned = [ours[0]] + arrived
    shared = [over_core(x, c) for c in range(PAIR) for x in owned]

    depth = stale.shape[0] // slabs
    held = lax.dynamic_slice_in_dim(stale, slab * depth, depth, axis=0)
    weight, *mine_out = merge_product(held, shared, pieces, heads)
    half = slabs // 2
    results = []
    for j in range(heads):
        if j == 0:
            parts = mine_out
        else:
            parts = []
            for group in (pieces[:half], pieces[half:]):
                moved = over_tensor(jnp.concatenate(group, axis=0), j)
                split = [moved[k * height : (k + 1) * height] for k in range(len(group))]
                parts += product(split, weight, not parts)
        total = parts[0] + bias[None, :]
        for k in range(1, slabs):
            total = total + over_slab(parts[k], k).astype(F32)
        results.append(total.astype(BF16))
    stacked = jnp.stack(results)
    if heads == 2:
        ordered = jnp.where(mine == 0, stacked, stacked[::-1])
    else:
        ordered = jnp.take(stacked, jnp.arange(heads) ^ mine, axis=0)
    projected = ordered.reshape(-1, stacked.shape[-1])
    return (new_first, new_second, projected)


def solution(mesh):
    rows = P(("dp", "tensor"), None)
    return jax.shard_map(
        on_device,
        mesh=mesh,
        in_specs=(rows, P(), P(None, "tensor"), P("tensor"), rows, rows, rows, rows, rows),
        out_specs=(rows, rows, P("dp", "tensor")),
        check_vma=False,
    )
```

```python
import functools

import jax
import jax.numpy as jnp
from jax import lax
from jax.experimental import pallas as pl
from jax.experimental.pallas import tpu as pltpu
from jax.sharding import PartitionSpec as P

PAIR = 2
CLIP = 448.0
MIB = 1024 * 1024
F32 = jnp.float32
BF16 = jnp.bfloat16
FAR = pl.BlockSpec(memory_space=pltpu.HBM)
NEAR = pl.BlockSpec(memory_space=pltpu.VMEM)
FREE = pl.CostEstimate(flops=0, bytes_accessed=0, transcendentals=0)


def far(x):
    return pltpu.with_memory_space_constraint(x, pltpu.HBM)


def near_by(x):
    return pltpu.with_memory_space_constraint(x, pltpu.VMEM)


def like(shape, dtype):
    return jax.ShapeDtypeStruct(shape, dtype)


def apart(m, core):
    return (m // 2) * 4 + core * 2 + m % 2


def norm_kernel(ours_ref, theirs_ref, gain_ref, *piece_refs):
    dp = lax.axis_index("dp")
    slab, core = dp // PAIR, dp % PAIR
    height = ours_ref.shape[0]
    width = piece_refs[0].shape[1]
    for turn, ref in enumerate((ours_ref, theirs_ref)):
        values = ref[...].astype(F32)
        scale = lax.rsqrt(jnp.mean(values * values, axis=1, keepdims=True) + 1e-06)
        rows = pl.ds(pl.multiple_of((core ^ turn) * height, height), height)
        for m, piece_ref in enumerate(piece_refs):
            columns = pl.ds(pl.multiple_of((slab ^ apart(m, core)) * width, width), width)
            piece_ref[rows, :] = (ref[:, columns].astype(F32) * scale * gain_ref[:, columns]).astype(BF16)


def norm(ours, theirs, gain, slabs):
    height, features = ours.shape
    return pl.pallas_call(
        norm_kernel,
        out_shape=[like((PAIR * height, features // slabs), BF16)] * (slabs // PAIR),
        compiler_params=pltpu.CompilerParams(vmem_limit_bytes=8 * MIB),
        cost_estimate=FREE,
    )(*[near_by(x) for x in (ours, theirs, gain.reshape(1, features))])


def adam_kernel(chunks, qrows, qcol, heads, *refs):
    expo_far, *inputs = refs[:5]
    new_first_out, new_second_out = refs[5:7]
    delta_outs = refs[7 : 7 + heads]
    b0, b1, b2, b3, n1, n2, expo_ref, sems, expo_sem = refs[7 + heads :]
    bufs = (b0, b1, b2, b3)
    mine = lax.axis_index("tensor")
    rows = inputs[0].shape[0]
    cols = inputs[0].shape[1] // heads
    groups = cols // qcol
    high = rows // chunks

    def window(j, c):
        head = mine ^ j
        return pl.ds(c * high, high), pl.ds(pl.multiple_of(head * cols, cols), cols)

    fetch_expo = pltpu.make_async_copy(expo_far, expo_ref, expo_sem)
    fetch_expo.start()
    steps = [(j, c) for j in range(heads) for c in range(chunks)]
    fetches, stores = [], []
    for n, (j, c) in enumerate(steps):
        here = (j, pl.ds(c * high, high), slice(None))
        at = window(j, c)
        fetches.append([pltpu.make_async_copy(inputs[a].at[at], bufs[a].at[here], sems.at[n, a]) for a in range(4)])
        for f in fetches[-1]:
            f.start()
    fetch_expo.wait()
    for n, (j, c) in enumerate(steps):
        head = mine ^ j
        for f in fetches[n]:
            f.wait()
        for b in range(high // qrows):
            row = c * (high // qrows) + b
            here = pl.ds(row * qrows, qrows)
            for g in range(groups):
                lanes = pl.ds(g * qcol, qcol)
                grad = b2[j, here, lanes]
                new_first = 0.9 * b0[j, here, lanes] + 0.1 * grad
                new_second = 0.95 * b1[j, here, lanes] + 0.05 * grad * grad
                n1[j, here, lanes] = new_first
                n2[j, here, lanes] = new_second
                bottom = new_second * lax.rsqrt(new_second) + 1e-08
                inverse = pl.reciprocal(bottom, approx=True)
                inverse = inverse * (2.0 - bottom * inverse)
                corrected = 0.02 * new_first * inverse + b3[j, here, lanes]
                expo = jnp.full((1, qcol), expo_ref[row, head * groups + g], jnp.int32).astype(F32)
                most = CLIP * jnp.exp2(-expo)
                delta_outs[j][here, lanes] = jnp.clip(corrected, -most, most).astype(BF16)
        at = window(j, c)
        here = (j, pl.ds(c * high, high), slice(None))
        stores += [
            pltpu.make_async_copy(n1.at[here], new_first_out.at[at], sems.at[n, 4]),
            pltpu.make_async_copy(n2.at[here], new_second_out.at[at], sems.at[n, 5]),
        ]
        for s in stores[-2:]:
            s.start()
    for s in stores:
        s.wait()


def adam(arrays, exponent, heads, chunks=2):
    rows, full = arrays[0].shape
    qrows, qcol = rows // exponent.shape[0], full // exponent.shape[1]
    cols = full // heads
    chunks = min(chunks, rows // qrows)
    return pl.pallas_call(
        functools.partial(adam_kernel, chunks, qrows, qcol, heads),
        in_specs=[FAR] * 5,
        out_specs=[FAR] * 2 + [NEAR] * heads,
        out_shape=[like((rows, full), F32)] * 2 + [like((rows, cols), BF16)] * heads,
        scratch_shapes=[pltpu.VMEM((heads, rows, cols), F32)] * 6
        + [
            pltpu.SMEM(exponent.shape, jnp.int32),
            pltpu.SemaphoreType.DMA((heads * chunks, 6)),
            pltpu.SemaphoreType.DMA(()),
        ],
        compiler_params=pltpu.CompilerParams(vmem_limit_bytes=20 * MIB),
        cost_estimate=FREE,
    )(*[far(x) for x in (exponent, *arrays)])


def place_rows(refs, heads, rows):
    core, mine = lax.axis_index("dp") % PAIR, lax.axis_index("tensor")
    for n, ref in enumerate(refs):
        at = ((core ^ (n // heads)) * heads + (mine ^ (n % heads))) * rows
        yield ref, pl.ds(pl.multiple_of(at, rows), rows)


def multiply(piece_refs, weight, out_refs):
    rows = out_refs[0].shape[0]
    stacked = jnp.concatenate([r[...] for r in piece_refs], axis=0)
    total = jnp.dot(stacked, weight, preferred_element_type=F32)
    for k, out_ref in enumerate(out_refs):
        out_ref[...] = total[k * rows : (k + 1) * rows].astype(out_ref.dtype)


def merge_kernel(slabs, heads, stale_ref, *refs):
    delta_refs, piece_refs = refs[: PAIR * heads], refs[PAIR * heads : PAIR * heads + slabs]
    weight_ref, out_refs = refs[PAIR * heads + slabs], refs[PAIR * heads + slabs + 1 :]
    for ref, here in place_rows(delta_refs, heads, delta_refs[0].shape[0]):
        weight_ref[here, :] = (stale_ref[here, :].astype(F32) + ref[...].astype(F32)).astype(BF16)
    multiply(piece_refs, weight_ref[...], out_refs)


def product_kernel(joined_ref, weight_ref, *out_refs):
    multiply([joined_ref], weight_ref[...], out_refs)


def merge_product(stale, deltas, pieces, heads, types):
    depth, cols = stale.shape
    return pl.pallas_call(
        functools.partial(merge_kernel, len(pieces), heads),
        out_shape=[like((depth, cols), BF16)] + [like((p.shape[0], cols), t) for p, t in zip(pieces, types)],
        compiler_params=pltpu.CompilerParams(vmem_limit_bytes=16 * MIB),
        cost_estimate=FREE,
    )(*[near_by(x) for x in (stale, *deltas, *pieces)])


def product(joined, weight, types):
    count = len(types)
    return pl.pallas_call(
        product_kernel,
        out_shape=[like((joined.shape[0] // count, weight.shape[1]), t) for t in types],
        compiler_params=pltpu.CompilerParams(vmem_limit_bytes=12 * MIB),
        cost_estimate=FREE,
    )(near_by(joined), near_by(weight))


def on_device(tokens, gain, stale, bias, first, second, grad, residual, exponent):
    heads = lax.axis_size("tensor")
    replicas = lax.axis_size("dp")
    slabs = replicas // PAIR
    partners = slabs // PAIR
    near, remote = range(partners // 2), range(partners // 2, partners)
    slab, core, mine = lax.axis_index("dp") // PAIR, lax.axis_index("dp") % PAIR, lax.axis_index("tensor")
    height = tokens.shape[0]

    def over_tensor(x, j):
        return x if j == 0 else lax.ppermute(x, "tensor", [(i, i ^ j) for i in range(heads)])

    def over_core(x):
        return lax.ppermute(x, "dp", [(i, i ^ 1) for i in range(replicas)])

    def over_slab(x, m):
        pairs = [(i, ((i // PAIR) ^ apart(m, i % PAIR)) * PAIR + i % PAIR) for i in range(replicas)]
        return lax.ppermute(x, "dp", pairs)

    def over_next(x):
        return lax.ppermute(x, "dp", [(i, i ^ PAIR) for i in range(replicas)])

    beside = over_core(tokens)
    new_first, new_second, *deltas = adam((first, second, grad, residual), exponent, heads)
    *deltas, beside = lax.optimization_barrier((*deltas, beside))
    owned = [over_tensor(deltas[j], j) for j in range(heads)]
    normed = norm(tokens, beside, gain, slabs)
    order = (*remote, *near)
    pieces = [over_slab(normed[m], m) for m in order]
    depth = stale.shape[0] // slabs
    held = lax.dynamic_slice_in_dim(stale, slab * depth, depth, axis=0)
    beside_ours = over_core(owned[0])
    held, pieces = lax.optimization_barrier((held, pieces))
    pieces = dict(zip(order, pieces))

    def over_heads(group):
        joined = jnp.concatenate([pieces[m] for m in group], axis=0)
        return [over_tensor(joined, j) for j in range(1, heads)]

    moved = over_heads(order)
    shared = owned + [beside_ours] + [over_core(x) for x in owned[1:]]
    def through_next(parts, group):
        met = over_next(jnp.concatenate(parts[1::2], axis=0))
        tall = parts[0].shape[0]
        sums = [(x + met[i * tall : (i + 1) * tall].astype(F32)).astype(BF16) for i, x in enumerate(parts[::2])]
        return [over_slab(x, m) for x, m in zip(sums, group[::2])]

    mixed = [F32, BF16] * (partners // 2)
    weight, *parts = merge_product(held, shared, [pieces[m] for m in order], heads, mixed)
    terms = [through_next(parts, order)]
    for j in range(1, heads):
        terms.append(through_next(product(moved[j - 1], weight, mixed), order))

    totals = [sum(x.astype(F32) for x in row).reshape(PAIR, height, -1) for row in terms]
    total = jnp.stack(totals, axis=1)
    keep = jnp.where(core == 0, total[0], total[1])
    give = jnp.where(core == 0, total[1], total[0])
    results = (keep + over_core(give) + bias).astype(BF16)
    if heads == 2:
        ordered = jnp.where(mine == 0, results, results[::-1])
    else:
        ordered = jnp.take(results, jnp.arange(heads) ^ mine, axis=0)
    projected = ordered.reshape(-1, results.shape[-1])
    return (new_first, new_second, projected)


def solution(mesh):
    rows = P(("dp", "tensor"), None)
    return jax.shard_map(
        on_device,
        mesh=mesh,
        in_specs=(rows, P(), P(None, "tensor"), P("tensor"), rows, rows, rows, rows, rows),
        out_specs=(rows, rows, P("dp", "tensor")),
        check_vma=False,
    )
```

```python
import functools

import jax
import jax.numpy as jnp
from jax import lax
from jax.experimental import pallas as pl
from jax.experimental.pallas import tpu as pltpu
from jax.sharding import PartitionSpec as P

PAIR = 2
CLIP = 448.0
MIB = 1024 * 1024
F32 = jnp.float32
BF16 = jnp.bfloat16
FAR = pl.BlockSpec(memory_space=pltpu.HBM)
NEAR = pl.BlockSpec(memory_space=pltpu.VMEM)
FREE = pl.CostEstimate(flops=0, bytes_accessed=0, transcendentals=0)


def far(x):
    return pltpu.with_memory_space_constraint(x, pltpu.HBM)


def near_by(x):
    return pltpu.with_memory_space_constraint(x, pltpu.VMEM)


def like(shape, dtype):
    return jax.ShapeDtypeStruct(shape, dtype)


def apart(m, core):
    return (m // 2) * 4 + core * 2 + m % 2


def norm_kernel(ours_ref, theirs_ref, gain_ref, *piece_refs):
    dp = lax.axis_index("dp")
    slab, core = dp // PAIR, dp % PAIR
    height = ours_ref.shape[0]
    width = piece_refs[0].shape[1]
    for turn, ref in enumerate((ours_ref, theirs_ref)):
        values = ref[...].astype(F32)
        scale = lax.rsqrt(jnp.mean(values * values, axis=1, keepdims=True) + 1e-06)
        rows = pl.ds(pl.multiple_of((core ^ turn) * height, height), height)
        for m, piece_ref in enumerate(piece_refs):
            columns = pl.ds(pl.multiple_of((slab ^ apart(m, core)) * width, width), width)
            piece_ref[rows, :] = (ref[:, columns].astype(F32) * scale * gain_ref[:, columns]).astype(BF16)


def norm(ours, theirs, gain, slabs):
    height, features = ours.shape
    return pl.pallas_call(
        norm_kernel,
        out_shape=[like((PAIR * height, features // slabs), BF16)] * (slabs // PAIR),
        compiler_params=pltpu.CompilerParams(vmem_limit_bytes=8 * MIB),
        cost_estimate=FREE,
    )(*[near_by(x) for x in (ours, theirs, gain.reshape(1, features))])


def step(first, second, grad):
    return 0.9 * first + 0.1 * grad, 0.95 * second + 0.05 * grad * grad


def delta_kernel(chunks, qrows, qcol, heads, start, count, *refs):
    expo_far, *inputs = refs[:5]
    delta_outs, (b0, b1, b2, b3, expo_ref, sems, expo_sem) = refs[5 : 5 + count], refs[5 + count :]
    bufs = (b0, b1, b2, b3)
    mine = lax.axis_index("tensor")
    rows = inputs[0].shape[0]
    cols = inputs[0].shape[1] // heads
    groups = cols // qcol
    high = rows // chunks
    fetch_expo = pltpu.make_async_copy(expo_far, expo_ref, expo_sem)
    fetch_expo.start()
    turns = [(j, c) for j in range(count) for c in range(chunks)]
    fetches = []
    for n, (j, c) in enumerate(turns):
        here = (j, pl.ds(c * high, high), slice(None))
        at = pl.ds(c * high, high), pl.ds(pl.multiple_of((mine ^ (start + j)) * cols, cols), cols)
        fetches.append([pltpu.make_async_copy(inputs[a].at[at], bufs[a].at[here], sems.at[n, a]) for a in range(4)])
        for f in fetches[-1]:
            f.start()
    fetch_expo.wait()
    for n, (j, c) in enumerate(turns):
        for f in fetches[n]:
            f.wait()
        for b in range(high // qrows):
            row = c * (high // qrows) + b
            here = pl.ds(row * qrows, qrows)
            for g in range(groups):
                lanes = pl.ds(g * qcol, qcol)
                new_first, new_second = step(b0[j, here, lanes], b1[j, here, lanes], b2[j, here, lanes])
                bottom = new_second * lax.rsqrt(new_second) + 1e-08
                inverse = pl.reciprocal(bottom, approx=True)
                inverse = inverse * (2.0 - bottom * inverse)
                corrected = 0.02 * new_first * inverse + b3[j, here, lanes]
                expo = jnp.full((1, qcol), expo_ref[row, (mine ^ (start + j)) * groups + g], jnp.int32).astype(F32)
                most = CLIP * jnp.exp2(-expo)
                delta_outs[j][here, lanes] = jnp.clip(corrected, -most, most).astype(BF16)


def delta(arrays, exponent, heads, start, count, chunks=2):
    rows, full = arrays[0].shape
    qrows, qcol = rows // exponent.shape[0], full // exponent.shape[1]
    cols = full // heads
    chunks = min(chunks, rows // qrows)
    return pl.pallas_call(
        functools.partial(delta_kernel, chunks, qrows, qcol, heads, start, count),
        in_specs=[FAR] * 5,
        out_specs=[NEAR] * count,
        out_shape=[like((rows, cols), BF16)] * count,
        scratch_shapes=[pltpu.VMEM((count, rows, cols), F32)] * 4
        + [
            pltpu.SMEM(exponent.shape, jnp.int32),
            pltpu.SemaphoreType.DMA((count * chunks, 4)),
            pltpu.SemaphoreType.DMA(()),
        ],
        compiler_params=pltpu.CompilerParams(vmem_limit_bytes=16 * MIB),
        cost_estimate=FREE,
    )(*[far(x) for x in (exponent, *arrays)])


def moments_kernel(chunks, *refs):
    inputs, outs, bufs, sems = refs[:3], refs[3:5], refs[5:10], refs[10]
    high = inputs[0].shape[0] // chunks
    at = [pl.ds(c * high, high) for c in range(chunks)]
    fetches = [[pltpu.make_async_copy(inputs[a].at[r], bufs[a].at[r], sems.at[c, a]) for a in range(3)] for c, r in enumerate(at)]
    stores = [[pltpu.make_async_copy(bufs[3 + a].at[r], outs[a].at[r], sems.at[c, 3 + a]) for a in range(2)] for c, r in enumerate(at)]
    for row in fetches:
        for f in row:
            f.start()
    for c, r in enumerate(at):
        for f in fetches[c]:
            f.wait()
        bufs[3][r, :], bufs[4][r, :] = step(bufs[0][r, :], bufs[1][r, :], bufs[2][r, :])
        for s in stores[c]:
            s.start()
    for row in stores:
        for s in row:
            s.wait()


def moments(first, second, grad, chunks=4):
    rows, full = first.shape
    chunks = min(chunks, rows // 8)
    return pl.pallas_call(
        functools.partial(moments_kernel, chunks),
        in_specs=[FAR] * 3,
        out_specs=[FAR] * 2,
        out_shape=[like((rows, full), F32)] * 2,
        scratch_shapes=[pltpu.VMEM((rows, full), F32)] * 5 + [pltpu.SemaphoreType.DMA((chunks, 5))],
        compiler_params=pltpu.CompilerParams(vmem_limit_bytes=16 * MIB),
        cost_estimate=pl.CostEstimate(flops=0, bytes_accessed=60 * rows * full, transcendentals=0),
    )(far(first), far(second), far(grad))


def multiply(piece_refs, weight, out_refs):
    rows = out_refs[0].shape[0]
    stacked = jnp.concatenate([r[...] for r in piece_refs], axis=0)
    total = jnp.dot(stacked, weight, preferred_element_type=F32)
    for k, out_ref in enumerate(out_refs):
        out_ref[...] = total[k * rows : (k + 1) * rows].astype(out_ref.dtype)


def merge_kernel(slabs, heads, stale_far, *refs):
    blocks = PAIR * heads
    delta_refs, piece_refs = refs[:blocks], refs[blocks : blocks + slabs]
    weight_ref, *out_refs, stale_ref, sems = refs[blocks + slabs :]
    dp, mine = lax.axis_index("dp"), lax.axis_index("tensor")
    rows = delta_refs[0].shape[0]
    fetches, places = [], []
    for n in range(blocks):
        at = ((dp % PAIR ^ (n // heads)) * heads + (mine ^ (n % heads))) * rows
        first = (dp // PAIR) * (blocks * rows) + at
        source = stale_far.at[pl.ds(pl.multiple_of(first, rows), rows), :]
        fetches.append(pltpu.make_async_copy(source, stale_ref.at[n], sems.at[n]))
        places.append(pl.ds(pl.multiple_of(at, rows), rows))
        fetches[-1].start()
    for n, here in enumerate(places):
        fetches[n].wait()
        weight_ref[here, :] = (stale_ref[n].astype(F32) + delta_refs[n][...].astype(F32)).astype(BF16)
    multiply(piece_refs, weight_ref[...], out_refs)


def product_kernel(groups, *refs):
    multiply(refs[:groups], refs[groups][...], refs[groups + 1 :])


def merge_product(stale, deltas, pieces, heads, types):
    rows, cols = deltas[0].shape
    blocks = len(deltas)
    return pl.pallas_call(
        functools.partial(merge_kernel, len(pieces), heads),
        in_specs=[FAR] + [NEAR] * (blocks + len(pieces)),
        out_shape=[like((blocks * rows, cols), BF16)]
        + [like((p.shape[0], cols), t) for p, t in zip(pieces, types)],
        scratch_shapes=[pltpu.VMEM((blocks, rows, cols), BF16), pltpu.SemaphoreType.DMA((blocks,))],
        compiler_params=pltpu.CompilerParams(vmem_limit_bytes=16 * MIB),
        cost_estimate=pl.CostEstimate(flops=0, bytes_accessed=8 * blocks * rows * cols, transcendentals=0),
    )(far(stale), *[near_by(x) for x in (*deltas, *pieces)])


def product(groups, weight, types):
    rows = sum(g.shape[0] for g in groups) // len(types)
    return pl.pallas_call(
        functools.partial(product_kernel, len(groups)),
        out_shape=[like((rows, weight.shape[1]), t) for t in types],
        compiler_params=pltpu.CompilerParams(vmem_limit_bytes=12 * MIB),
        cost_estimate=FREE,
    )(*[near_by(x) for x in (*groups, weight)])


def on_device(tokens, gain, stale, bias, first, second, grad, residual, exponent):
    heads = lax.axis_size("tensor")
    replicas = lax.axis_size("dp")
    slabs = replicas // PAIR
    partners = slabs // PAIR
    near, remote = range(partners // 2), range(partners // 2, partners)
    core, mine = lax.axis_index("dp") % PAIR, lax.axis_index("tensor")
    height = tokens.shape[0]

    def over_tensor(x, j):
        return x if j == 0 else lax.ppermute(x, "tensor", [(i, i ^ j) for i in range(heads)])

    def over_core(x):
        return lax.ppermute(x, "dp", [(i, i ^ 1) for i in range(replicas)])

    def over_slab(x, m):
        pairs = [(i, ((i // PAIR) ^ apart(m, i % PAIR)) * PAIR + i % PAIR) for i in range(replicas)]
        return lax.ppermute(x, "dp", pairs)

    def over_next(x):
        return lax.ppermute(x, "dp", [(i, i ^ PAIR) for i in range(replicas)])

    beside = over_core(tokens)
    arrays = (first, second, grad, residual)
    theirs = delta(arrays, exponent, heads, 1, heads - 1)
    theirs, beside = lax.optimization_barrier((theirs, beside))
    arrived = [over_tensor(theirs[j], j + 1) for j in range(heads - 1)]
    normed = norm(tokens, beside, gain, slabs)
    order = (*remote, *near)
    pieces = [over_slab(normed[m], m) for m in order]
    exponent, normed = lax.optimization_barrier((exponent, normed))
    ours = delta(arrays, exponent, heads, 0, 1)
    distant, close = pieces[: len(remote)], pieces[len(remote) :]

    def over_heads(group):
        return [[over_tensor(x, j) for x in group] for j in range(1, heads)]

    ours, close = lax.optimization_barrier((ours, close))
    moved_close = over_heads(close)
    distant, arrived, moved_close = lax.optimization_barrier((distant, arrived, moved_close))
    moved_distant = over_heads([jnp.concatenate(distant, axis=0)])
    shared = [*ours, *arrived]
    shared = shared + [over_core(x) for x in shared]
    pieces = dict(zip(order, (*distant, *close)))

    def added(parts, met):
        tall = parts[0].shape[0]
        return [(x + met[i * tall : (i + 1) * tall].astype(F32)).astype(BF16) for i, x in enumerate(parts[::2])]

    mixed = [F32, BF16] * (partners // 2)
    weight, *parts = merge_product(stale, shared, [pieces[m] for m in order], heads, mixed)
    met = over_next(jnp.concatenate(parts[1::2], axis=0))
    met, moved_distant = lax.optimization_barrier((met, moved_distant))
    rows = [(parts, met)]
    for j in range(1, heads):
        parts = product([*moved_distant[j - 1], *moved_close[j - 1]], weight, mixed)
        rows.append((parts, over_next(jnp.concatenate(parts[1::2], axis=0))))
    terms = [[over_slab(x, m) for x, m in zip(added(*row), order[::2])] for row in rows]
    new_first, new_second = moments(first, second, grad)
    new_first, new_second, terms = lax.optimization_barrier((new_first, new_second, terms))

    totals = [sum(x.astype(F32) for x in row).reshape(PAIR, height, -1) for row in terms]
    total = jnp.stack(totals, axis=1)
    keep = jnp.where(core == 0, total[0], total[1])
    give = jnp.where(core == 0, total[1], total[0])
    results = (keep + over_core(give) + bias).astype(BF16)
    if heads == 2:
        ordered = jnp.where(mine == 0, results, results[::-1])
    else:
        ordered = jnp.take(results, jnp.arange(heads) ^ mine, axis=0)
    projected = ordered.reshape(-1, results.shape[-1])
    return (new_first, new_second, projected)


def solution(mesh):
    rows = P(("dp", "tensor"), None)
    return jax.shard_map(
        on_device,
        mesh=mesh,
        in_specs=(rows, P(), P(None, "tensor"), P("tensor"), rows, rows, rows, rows, rows),
        out_specs=(rows, rows, P("dp", "tensor")),
        check_vma=False,
    )
```

```python
import functools

import jax
import jax.numpy as jnp
from jax import lax
from jax.experimental import pallas as pl
from jax.experimental.pallas import tpu as pltpu
from jax.sharding import PartitionSpec as P

PAIR = 2
CLIP = 448.0
MIB = 1024 * 1024
F32 = jnp.float32
BF16 = jnp.bfloat16
FAR = pl.BlockSpec(memory_space=pltpu.HBM)
NEAR = pl.BlockSpec(memory_space=pltpu.VMEM)
FREE = pl.CostEstimate(flops=0, bytes_accessed=0, transcendentals=0)


def far(x):
    return pltpu.with_memory_space_constraint(x, pltpu.HBM)


def near_by(x):
    return pltpu.with_memory_space_constraint(x, pltpu.VMEM)


def like(shape, dtype):
    return jax.ShapeDtypeStruct(shape, dtype)


def apart(m, core):
    return (m // 2) * 4 + core * 2 + m % 2


def norm_kernel(ours_ref, theirs_ref, gain_ref, *piece_refs):
    dp = lax.axis_index("dp")
    slab, core = dp // PAIR, dp % PAIR
    height = ours_ref.shape[0]
    width = piece_refs[0].shape[1]
    for turn, ref in enumerate((ours_ref, theirs_ref)):
        values = ref[...].astype(F32)
        scale = lax.rsqrt(jnp.mean(values * values, axis=1, keepdims=True) + 1e-06)
        rows = pl.ds(pl.multiple_of((core ^ turn) * height, height), height)
        for m, piece_ref in enumerate(piece_refs):
            columns = pl.ds(pl.multiple_of((slab ^ apart(m, core)) * width, width), width)
            piece_ref[rows, :] = (ref[:, columns].astype(F32) * scale * gain_ref[:, columns]).astype(BF16)


def norm(ours, theirs, gain, slabs):
    height, features = ours.shape
    return pl.pallas_call(
        norm_kernel,
        out_shape=[like((PAIR * height, features // slabs), BF16)] * (slabs // PAIR),
        compiler_params=pltpu.CompilerParams(vmem_limit_bytes=8 * MIB),
        cost_estimate=FREE,
    )(*[near_by(x) for x in (ours, theirs, gain.reshape(1, features))])


def step(first, second, grad):
    return 0.9 * first + 0.1 * grad, 0.95 * second + 0.05 * grad * grad


def delta_kernel(chunks, qrows, qcol, heads, start, count, *refs):
    expo_far, *inputs = refs[:5]
    delta_outs, (b0, b1, b2, b3, expo_ref, sems, expo_sem) = refs[5 : 5 + count], refs[5 + count :]
    bufs = (b0, b1, b2, b3)
    mine = lax.axis_index("tensor")
    rows = inputs[0].shape[0]
    cols = inputs[0].shape[1] // heads
    groups = cols // qcol
    high = rows // chunks
    fetch_expo = pltpu.make_async_copy(expo_far, expo_ref, expo_sem)
    fetch_expo.start()
    turns = [(j, c) for j in range(count) for c in range(chunks)]
    fetches = []
    for n, (j, c) in enumerate(turns):
        here = (j, pl.ds(c * high, high), slice(None))
        at = pl.ds(c * high, high), pl.ds(pl.multiple_of((mine ^ (start + j)) * cols, cols), cols)
        fetches.append([pltpu.make_async_copy(inputs[a].at[at], bufs[a].at[here], sems.at[n, a]) for a in range(4)])
        for f in fetches[-1]:
            f.start()
    fetch_expo.wait()
    for n, (j, c) in enumerate(turns):
        for f in fetches[n]:
            f.wait()
        for b in range(high // qrows):
            row = c * (high // qrows) + b
            here = pl.ds(row * qrows, qrows)
            for g in range(groups):
                lanes = pl.ds(g * qcol, qcol)
                new_first, new_second = step(b0[j, here, lanes], b1[j, here, lanes], b2[j, here, lanes])
                bottom = new_second * lax.rsqrt(new_second) + 1e-08
                inverse = pl.reciprocal(bottom, approx=True)
                inverse = inverse * (2.0 - bottom * inverse)
                corrected = 0.02 * new_first * inverse + b3[j, here, lanes]
                expo = jnp.full((1, qcol), expo_ref[row, (mine ^ (start + j)) * groups + g], jnp.int32).astype(F32)
                most = CLIP * jnp.exp2(-expo)
                delta_outs[j][here, lanes] = jnp.clip(corrected, -most, most).astype(BF16)


def delta(arrays, exponent, heads, start, count, chunks=2):
    rows, full = arrays[0].shape
    qrows, qcol = rows // exponent.shape[0], full // exponent.shape[1]
    cols = full // heads
    chunks = min(chunks, rows // qrows)
    return pl.pallas_call(
        functools.partial(delta_kernel, chunks, qrows, qcol, heads, start, count),
        in_specs=[FAR] * 5,
        out_specs=[NEAR] * count,
        out_shape=[like((rows, cols), BF16)] * count,
        scratch_shapes=[pltpu.VMEM((count, rows, cols), F32)] * 4
        + [
            pltpu.SMEM(exponent.shape, jnp.int32),
            pltpu.SemaphoreType.DMA((count * chunks, 4)),
            pltpu.SemaphoreType.DMA(()),
        ],
        compiler_params=pltpu.CompilerParams(vmem_limit_bytes=16 * MIB),
        cost_estimate=FREE,
    )(*[far(x) for x in (exponent, *arrays)])


def moments_kernel(chunks, *refs):
    inputs, outs, bufs, sems = refs[:3], refs[3:5], refs[5:10], refs[10]
    high = inputs[0].shape[0] // chunks
    at = [pl.ds(c * high, high) for c in range(chunks)]
    fetches = [[pltpu.make_async_copy(inputs[a].at[r], bufs[a].at[r], sems.at[c, a]) for a in range(3)] for c, r in enumerate(at)]
    stores = [[pltpu.make_async_copy(bufs[3 + a].at[r], outs[a].at[r], sems.at[c, 3 + a]) for a in range(2)] for c, r in enumerate(at)]
    for row in fetches:
        for f in row:
            f.start()
    for c, r in enumerate(at):
        for f in fetches[c]:
            f.wait()
        bufs[3][r, :], bufs[4][r, :] = step(bufs[0][r, :], bufs[1][r, :], bufs[2][r, :])
        for s in stores[c]:
            s.start()
    for row in stores:
        for s in row:
            s.wait()


def moments(first, second, grad, chunks=4):
    rows, full = first.shape
    chunks = min(chunks, rows // 8)
    return pl.pallas_call(
        functools.partial(moments_kernel, chunks),
        in_specs=[FAR] * 3,
        out_specs=[FAR] * 2,
        out_shape=[like((rows, full), F32)] * 2,
        scratch_shapes=[pltpu.VMEM((rows, full), F32)] * 5 + [pltpu.SemaphoreType.DMA((chunks, 5))],
        compiler_params=pltpu.CompilerParams(vmem_limit_bytes=16 * MIB),
        cost_estimate=pl.CostEstimate(flops=0, bytes_accessed=60 * rows * full, transcendentals=0),
    )(far(first), far(second), far(grad))


def multiply(piece_refs, labels, weight, plan, out_refs):
    stacked = jnp.concatenate([r[...] for r in piece_refs], axis=0)
    total = jnp.dot(stacked, weight, preferred_element_type=F32)
    tall = total.shape[0] // len(labels)
    for wanted, out_ref in zip(plan, out_refs):
        for n, label in enumerate(wanted):
            at = labels.index(label) * tall
            out_ref[n * tall : (n + 1) * tall, :] = total[at : at + tall].astype(out_ref.dtype)


def joined(tall, cols, plan, types):
    return [like((len(wanted) * tall, cols), t) for wanted, t in zip(plan, types)]


def merge_kernel(heads, labels, plan, stale_far, *refs):
    blocks = PAIR * heads
    delta_refs, piece_refs = refs[:blocks], refs[blocks : -(len(plan) + 3)]
    weight_ref, *out_refs, stale_ref, sems = refs[-(len(plan) + 3) :]
    dp, mine = lax.axis_index("dp"), lax.axis_index("tensor")
    rows = delta_refs[0].shape[0]
    fetches, places = [], []
    for n in range(blocks):
        at = ((dp % PAIR ^ (n // heads)) * heads + (mine ^ (n % heads))) * rows
        first = (dp // PAIR) * (blocks * rows) + at
        source = stale_far.at[pl.ds(pl.multiple_of(first, rows), rows), :]
        fetches.append(pltpu.make_async_copy(source, stale_ref.at[n], sems.at[n]))
        places.append(pl.ds(pl.multiple_of(at, rows), rows))
        fetches[-1].start()
    for n, here in enumerate(places):
        fetches[n].wait()
        weight_ref[here, :] = (stale_ref[n].astype(F32) + delta_refs[n][...].astype(F32)).astype(BF16)
    multiply(piece_refs, labels, weight_ref[...], plan, out_refs)


def product_kernel(labels, plan, *refs):
    *piece_refs, weight_ref = refs[: -len(plan)]
    multiply(piece_refs, labels, weight_ref[...], plan, refs[-len(plan) :])


def merge_product(stale, deltas, pieces, heads, labels, plan, types):
    rows, cols = deltas[0].shape
    blocks = len(deltas)
    tall = sum(p.shape[0] for p in pieces) // len(labels)
    return pl.pallas_call(
        functools.partial(merge_kernel, heads, labels, plan),
        in_specs=[FAR] + [NEAR] * (blocks + len(pieces)),
        out_shape=[like((blocks * rows, cols), BF16)] + joined(tall, cols, plan, types),
        scratch_shapes=[pltpu.VMEM((blocks, rows, cols), BF16), pltpu.SemaphoreType.DMA((blocks,))],
        compiler_params=pltpu.CompilerParams(vmem_limit_bytes=16 * MIB),
        cost_estimate=pl.CostEstimate(flops=0, bytes_accessed=8 * blocks * rows * cols, transcendentals=0),
    )(far(stale), *[near_by(x) for x in (*deltas, *pieces)])


def product(pieces, weight, labels, plan, types):
    tall = sum(p.shape[0] for p in pieces) // len(labels)
    return pl.pallas_call(
        functools.partial(product_kernel, labels, plan),
        out_shape=joined(tall, weight.shape[1], plan, types),
        compiler_params=pltpu.CompilerParams(vmem_limit_bytes=12 * MIB),
        cost_estimate=FREE,
    )(*[near_by(x) for x in (*pieces, weight)])


def on_device(tokens, gain, stale, bias, first, second, grad, residual, exponent):
    heads = lax.axis_size("tensor")
    replicas = lax.axis_size("dp")
    slabs = replicas // PAIR
    partners = slabs // PAIR
    near, remote = range(partners // 2), range(partners // 2, partners)
    core, mine = lax.axis_index("dp") % PAIR, lax.axis_index("tensor")
    height = tokens.shape[0]

    def over_tensor(x, j):
        return x if j == 0 else lax.ppermute(x, "tensor", [(i, i ^ j) for i in range(heads)])

    def over_core(x):
        return lax.ppermute(x, "dp", [(i, i ^ 1) for i in range(replicas)])

    def over_slab(x, m):
        pairs = [(i, ((i // PAIR) ^ apart(m, i % PAIR)) * PAIR + i % PAIR) for i in range(replicas)]
        return lax.ppermute(x, "dp", pairs)

    def over_next(x):
        return lax.ppermute(x, "dp", [(i, i ^ PAIR) for i in range(replicas)])

    beside = over_core(tokens)
    arrays = (first, second, grad, residual)
    theirs = delta(arrays, exponent, heads, 1, heads - 1)
    theirs, beside = lax.optimization_barrier((theirs, beside))
    arrived = [over_tensor(theirs[j], j + 1) for j in range(heads - 1)]
    normed = norm(tokens, beside, gain, slabs)
    order = (*remote, *near)
    pieces = [over_slab(normed[m], m) for m in order]
    exponent, normed = lax.optimization_barrier((exponent, normed))
    ours = delta(arrays, exponent, heads, 0, 1)
    distant, close = pieces[: len(remote)], pieces[len(remote) :]

    def over_heads(group):
        return [[over_tensor(x, j) for x in group] for j in range(1, heads)]

    ours, close = lax.optimization_barrier((ours, close))
    moved_close = over_heads(close)
    distant, arrived, moved_close = lax.optimization_barrier((distant, arrived, moved_close))
    moved_distant = over_heads([jnp.concatenate(distant, axis=0)])
    shared = [*ours, *arrived]
    shared = shared + [over_core(x) for x in shared]
    peers = range(1, heads)
    evens, odds = remote[::2], remote[1::2]
    labels = [(0, m) for m in order] + [(j, m) for j in peers for m in near]
    plan = [[(0, m)] for m in (*evens, *odds)] + [[(j, m) for j in range(heads)] for m in near]
    types = [F32] * len(evens) + [BF16] * (len(odds) + len(near))
    blocks = [*distant, *close, *[x for row in moved_close for x in row]]
    weight, *parts = merge_product(stale, shared, blocks, heads, labels, plan, types)
    ours_even, ours_odd, parts_near = parts[: len(evens)], parts[len(evens) : len(remote)], parts[len(remote) :]
    met = [over_next(x) for x in ours_odd]
    terms_near = [over_slab(x, m) for x, m in zip(parts_near, near)]
    met, moved_distant = lax.optimization_barrier((met, moved_distant))

    labels = [(j, m) for j in peers for m in remote]
    plan = [[(j, m) for j in peers] for m in (*evens, *odds)]
    parts = product([x for row in moved_distant for x in row], weight, labels, plan, types[: len(remote)])
    theirs_even, theirs_odd = parts[: len(evens)], parts[len(evens) :]
    met_theirs = [over_next(x) for x in theirs_odd]

    def onward(even, arrived):
        return [over_slab((x + y.astype(F32)).astype(BF16), m) for x, y, m in zip(even, arrived, evens)]

    terms_ours = onward(ours_even, met)
    terms_theirs = onward(theirs_even, met_theirs)
    new_first, new_second = moments(first, second, grad)
    new_first, new_second, terms_near, terms_ours, terms_theirs = lax.optimization_barrier(
        (new_first, new_second, terms_near, terms_ours, terms_theirs)
    )

    def added(terms):
        return sum(x.astype(F32) for x in terms).reshape(-1, PAIR, height, weight.shape[1])

    total = added(terms_near) + jnp.concatenate([added(terms_ours), added(terms_theirs)], axis=0)
    keep = jnp.where(core == 0, total[:, 0], total[:, 1])
    give = jnp.where(core == 0, total[:, 1], total[:, 0])
    results = (keep + over_core(give) + bias).astype(BF16)
    if heads == 2:
        ordered = jnp.where(mine == 0, results, results[::-1])
    else:
        ordered = jnp.take(results, jnp.arange(heads) ^ mine, axis=0)
    projected = ordered.reshape(-1, results.shape[-1])
    return (new_first, new_second, projected)


def solution(mesh):
    rows = P(("dp", "tensor"), None)
    return jax.shard_map(
        on_device,
        mesh=mesh,
        in_specs=(rows, P(), P(None, "tensor"), P("tensor"), rows, rows, rows, rows, rows),
        out_specs=(rows, rows, P("dp", "tensor")),
        check_vma=False,
    )
```

```python
import functools

import jax
import jax.numpy as jnp
from jax import lax
from jax.experimental import pallas as pl
from jax.experimental.pallas import tpu as pltpu
from jax.sharding import PartitionSpec as P

PAIR = 2
CLIP = 448.0
MIB = 1024 * 1024
F32 = jnp.float32
BF16 = jnp.bfloat16
FAR = pl.BlockSpec(memory_space=pltpu.HBM)
NEAR = pl.BlockSpec(memory_space=pltpu.VMEM)
FREE = pl.CostEstimate(flops=0, bytes_accessed=0, transcendentals=0)


def far(x):
    return pltpu.with_memory_space_constraint(x, pltpu.HBM)


def near_by(x):
    return pltpu.with_memory_space_constraint(x, pltpu.VMEM)


def like(shape, dtype):
    return jax.ShapeDtypeStruct(shape, dtype)


def apart(m, core):
    return (m // 2) * 4 + core * 2 + m % 2


def norm_kernel(ours_ref, theirs_ref, gain_ref, *piece_refs):
    dp = lax.axis_index("dp")
    slab, core = dp // PAIR, dp % PAIR
    height = ours_ref.shape[0]
    width = piece_refs[0].shape[1]
    for turn, ref in enumerate((ours_ref, theirs_ref)):
        values = ref[...].astype(F32)
        scale = lax.rsqrt(jnp.mean(values * values, axis=1, keepdims=True) + 1e-06)
        rows = pl.ds(pl.multiple_of((core ^ turn) * height, height), height)
        for m, piece_ref in enumerate(piece_refs):
            columns = pl.ds(pl.multiple_of((slab ^ apart(m, core)) * width, width), width)
            piece_ref[rows, :] = (ref[:, columns].astype(F32) * scale * gain_ref[:, columns]).astype(BF16)


def norm(ours, theirs, gain, slabs):
    height, features = ours.shape
    return pl.pallas_call(
        norm_kernel,
        out_shape=[like((PAIR * height, features // slabs), BF16)] * (slabs // PAIR),
        compiler_params=pltpu.CompilerParams(vmem_limit_bytes=8 * MIB),
        cost_estimate=FREE,
    )(*[near_by(x) for x in (ours, theirs, gain.reshape(1, features))])


def step(first, second, grad):
    return 0.9 * first + 0.1 * grad, 0.95 * second + 0.05 * grad * grad


def delta_kernel(chunks, qrows, qcol, heads, start, count, *refs):
    expo_far, *inputs = refs[:5]
    delta_outs, (b0, b1, b2, b3, expo_ref, sems, expo_sem) = refs[5 : 5 + count], refs[5 + count :]
    bufs = (b0, b1, b2, b3)
    mine = lax.axis_index("tensor")
    rows = inputs[0].shape[0]
    cols = inputs[0].shape[1] // heads
    groups = cols // qcol
    high = rows // chunks
    fetch_expo = pltpu.make_async_copy(expo_far, expo_ref, expo_sem)
    fetch_expo.start()
    turns = [(j, c) for j in range(count) for c in range(chunks)]
    fetches = []
    for n, (j, c) in enumerate(turns):
        here = (j, pl.ds(c * high, high), slice(None))
        at = pl.ds(c * high, high), pl.ds(pl.multiple_of((mine ^ (start + j)) * cols, cols), cols)
        fetches.append([pltpu.make_async_copy(inputs[a].at[at], bufs[a].at[here], sems.at[n, a]) for a in range(4)])
        for f in fetches[-1]:
            f.start()
    fetch_expo.wait()
    for n, (j, c) in enumerate(turns):
        for f in fetches[n]:
            f.wait()
        for b in range(high // qrows):
            row = c * (high // qrows) + b
            here = pl.ds(row * qrows, qrows)
            for g in range(groups):
                lanes = pl.ds(g * qcol, qcol)
                new_first, new_second = step(b0[j, here, lanes], b1[j, here, lanes], b2[j, here, lanes])
                bottom = new_second * lax.rsqrt(new_second) + 1e-08
                inverse = pl.reciprocal(bottom, approx=True)
                inverse = inverse * (2.0 - bottom * inverse)
                corrected = 0.02 * new_first * inverse + b3[j, here, lanes]
                expo = jnp.full((1, qcol), expo_ref[row, (mine ^ (start + j)) * groups + g], jnp.int32).astype(F32)
                most = CLIP * jnp.exp2(-expo)
                delta_outs[j][here, lanes] = jnp.clip(corrected, -most, most).astype(BF16)


def delta(arrays, exponent, heads, start, count, chunks=2):
    rows, full = arrays[0].shape
    qrows, qcol = rows // exponent.shape[0], full // exponent.shape[1]
    cols = full // heads
    chunks = min(chunks, rows // qrows)
    return pl.pallas_call(
        functools.partial(delta_kernel, chunks, qrows, qcol, heads, start, count),
        in_specs=[FAR] * 5,
        out_specs=[NEAR] * count,
        out_shape=[like((rows, cols), BF16)] * count,
        scratch_shapes=[pltpu.VMEM((count, rows, cols), F32)] * 4
        + [
            pltpu.SMEM(exponent.shape, jnp.int32),
            pltpu.SemaphoreType.DMA((count * chunks, 4)),
            pltpu.SemaphoreType.DMA(()),
        ],
        compiler_params=pltpu.CompilerParams(vmem_limit_bytes=16 * MIB),
        cost_estimate=FREE,
    )(*[far(x) for x in (exponent, *arrays)])


def moments_kernel(start, size, chunks, *refs):
    inputs, outs, bufs, sems = refs[:3], refs[-8:-6], refs[-6:-1], refs[-1]
    high = size // chunks
    turns = [(pl.ds(start + c * high, high), pl.ds(c * high, high)) for c in range(chunks)]
    fetches = [
        [pltpu.make_async_copy(inputs[a].at[there], bufs[a].at[here], sems.at[c, a]) for a in range(3)]
        for c, (there, here) in enumerate(turns)
    ]
    stores = [
        [pltpu.make_async_copy(bufs[3 + a].at[here], outs[a].at[there], sems.at[c, 3 + a]) for a in range(2)]
        for c, (there, here) in enumerate(turns)
    ]
    for row in fetches:
        for f in row:
            f.start()
    for c, (_, here) in enumerate(turns):
        for f in fetches[c]:
            f.wait()
        bufs[3][here, :], bufs[4][here, :] = step(bufs[0][here, :], bufs[1][here, :], bufs[2][here, :])
        for s in stores[c]:
            s.start()
    for row in stores:
        for s in row:
            s.wait()


def moments(arrays, start, size, made=(), chunks=4):
    rows, full = arrays[0].shape
    chunks = min(chunks, size // 8)
    return pl.pallas_call(
        functools.partial(moments_kernel, start, size, chunks),
        in_specs=[FAR] * (3 + len(made)),
        out_specs=[FAR] * 2,
        out_shape=[like((rows, full), F32)] * 2,
        scratch_shapes=[pltpu.VMEM((size, full), F32)] * 5 + [pltpu.SemaphoreType.DMA((chunks, 5))],
        input_output_aliases={3 + i: i for i in range(len(made))},
        compiler_params=pltpu.CompilerParams(vmem_limit_bytes=16 * MIB),
        cost_estimate=pl.CostEstimate(flops=0, bytes_accessed=60 * rows * full, transcendentals=0),
    )(*[far(x) for x in (*arrays, *made)])


def multiply(piece_refs, labels, weight, plan, out_refs):
    stacked = jnp.concatenate([r[...] for r in piece_refs], axis=0)
    total = jnp.dot(stacked, weight, preferred_element_type=F32)
    tall = total.shape[0] // len(labels)
    for wanted, out_ref in zip(plan, out_refs):
        for n, label in enumerate(wanted):
            at = labels.index(label) * tall
            out_ref[n * tall : (n + 1) * tall, :] = total[at : at + tall].astype(out_ref.dtype)


def joined(tall, cols, plan, types):
    return [like((len(wanted) * tall, cols), t) for wanted, t in zip(plan, types)]


def places(heads, rows):
    core, mine = lax.axis_index("dp") % PAIR, lax.axis_index("tensor")
    for n in range(PAIR * heads):
        yield ((core ^ (n // heads)) * heads + (mine ^ (n % heads))) * rows


def fetch_kernel(heads, stale_far, out_ref, sems):
    blocks, rows = out_ref.shape[:2]
    copies = []
    for n, at in enumerate(places(heads, rows)):
        first = (lax.axis_index("dp") // PAIR) * (blocks * rows) + at
        source = stale_far.at[pl.ds(pl.multiple_of(first, rows), rows), :]
        copies.append(pltpu.make_async_copy(source, out_ref.at[n], sems.at[n]))
        copies[-1].start()
    for copy in copies:
        copy.wait()


def fetch(stale, heads, slabs):
    blocks = PAIR * heads
    return pl.pallas_call(
        functools.partial(fetch_kernel, heads),
        in_specs=[FAR],
        out_specs=NEAR,
        out_shape=like((blocks, stale.shape[0] // slabs // blocks, stale.shape[1]), BF16),
        scratch_shapes=[pltpu.SemaphoreType.DMA((blocks,))],
        compiler_params=pltpu.CompilerParams(vmem_limit_bytes=8 * MIB),
        cost_estimate=FREE,
    )(far(stale))


def merge_kernel(heads, labels, plan, stale_ref, *refs):
    blocks = PAIR * heads
    delta_refs, piece_refs = refs[:blocks], refs[blocks : -(len(plan) + 1)]
    weight_ref, *out_refs = refs[-(len(plan) + 1) :]
    rows = delta_refs[0].shape[0]
    for n, at in enumerate(places(heads, rows)):
        here = pl.ds(pl.multiple_of(at, rows), rows)
        weight_ref[here, :] = (stale_ref[n].astype(F32) + delta_refs[n][...].astype(F32)).astype(BF16)
    multiply(piece_refs, labels, weight_ref[...], plan, out_refs)


def product_kernel(labels, plan, *refs):
    *piece_refs, weight_ref = refs[: -len(plan)]
    multiply(piece_refs, labels, weight_ref[...], plan, refs[-len(plan) :])


def merge_product(stale, deltas, pieces, heads, labels, plan, types):
    rows, cols = deltas[0].shape
    blocks = len(deltas)
    tall = sum(p.shape[0] for p in pieces) // len(labels)
    return pl.pallas_call(
        functools.partial(merge_kernel, heads, labels, plan),
        out_shape=[like((blocks * rows, cols), BF16)] + joined(tall, cols, plan, types),
        compiler_params=pltpu.CompilerParams(vmem_limit_bytes=16 * MIB),
        cost_estimate=pl.CostEstimate(flops=0, bytes_accessed=8 * blocks * rows * cols, transcendentals=0),
    )(*[near_by(x) for x in (stale, *deltas, *pieces)])


def product(pieces, weight, labels, plan, types):
    tall = sum(p.shape[0] for p in pieces) // len(labels)
    return pl.pallas_call(
        functools.partial(product_kernel, labels, plan),
        out_shape=joined(tall, weight.shape[1], plan, types),
        compiler_params=pltpu.CompilerParams(vmem_limit_bytes=12 * MIB),
        cost_estimate=FREE,
    )(*[near_by(x) for x in (*pieces, weight)])


def on_device(tokens, gain, stale, bias, first, second, grad, residual, exponent):
    heads = lax.axis_size("tensor")
    replicas = lax.axis_size("dp")
    slabs = replicas // PAIR
    partners = slabs // PAIR
    near, remote = range(partners // 2), range(partners // 2, partners)
    core, mine = lax.axis_index("dp") % PAIR, lax.axis_index("tensor")
    height = tokens.shape[0]

    def over_tensor(x, j):
        return x if j == 0 else lax.ppermute(x, "tensor", [(i, i ^ j) for i in range(heads)])

    def over_core(x):
        return lax.ppermute(x, "dp", [(i, i ^ 1) for i in range(replicas)])

    def over_slab(x, m):
        pairs = [(i, ((i // PAIR) ^ apart(m, i % PAIR)) * PAIR + i % PAIR) for i in range(replicas)]
        return lax.ppermute(x, "dp", pairs)

    def over_next(x):
        return lax.ppermute(x, "dp", [(i, i ^ PAIR) for i in range(replicas)])

    beside = over_core(tokens)
    arrays = (first, second, grad, residual)
    theirs = delta(arrays, exponent, heads, 1, heads - 1)
    theirs, beside = lax.optimization_barrier((theirs, beside))
    arrived = [over_tensor(theirs[j], j + 1) for j in range(heads - 1)]
    normed = norm(tokens, beside, gain, slabs)
    order = (*remote, *near)
    pieces = [over_slab(normed[m], m) for m in order]
    exponent, normed = lax.optimization_barrier((exponent, normed))
    ours = delta(arrays, exponent, heads, 0, 1)
    distant, close = pieces[: len(remote)], pieces[len(remote) :]

    def over_heads(group):
        return [[over_tensor(x, j) for x in group] for j in range(1, heads)]

    ours, close = lax.optimization_barrier((ours, close))
    moved_close = over_heads(close)
    first_rows = first.shape[0]
    bulk = first_rows // 2
    made = moments(arrays[:3], 0, bulk)
    held = fetch(stale, heads, slabs)
    made, held, distant, arrived, moved_close = lax.optimization_barrier((made, held, distant, arrived, moved_close))
    moved_distant = over_heads([jnp.concatenate(distant, axis=0)])
    shared = [*ours, *arrived]
    shared = shared + [over_core(x) for x in shared]
    peers = range(1, heads)
    evens, odds = remote[::2], remote[1::2]
    labels = [(0, m) for m in order] + [(j, m) for j in peers for m in near]
    plan = [[(0, m)] for m in (*evens, *odds)] + [[(j, m) for j in range(heads)] for m in near[::2]]
    plan += [[(j, m) for j in group] for group in ([0], peers) for m in near[1::2]]
    types = [F32] * len(evens) + [BF16] * (len(odds) + len(near) + len(near[1::2]))
    blocks = [*distant, *close, *[x for row in moved_close for x in row]]
    weight, *parts = merge_product(held, shared, blocks, heads, labels, plan, types)
    ours_even, ours_odd, parts_near = parts[: len(evens)], parts[len(evens) : len(remote)], parts[len(remote) :]
    met = [over_next(x) for x in ours_odd]
    split = len(near[::2])
    last = split + len(near[1::2])
    terms_near = [over_slab(x, m) for x, m in zip(parts_near[:split], near[::2])]
    terms_ours = [over_slab(x, m) for x, m in zip(parts_near[split:last], near[1::2])]
    late = parts_near[last:]
    met, moved_distant = lax.optimization_barrier((met, moved_distant))

    labels = [(j, m) for j in peers for m in remote]
    plan = [[(j, m) for j in peers] for m in (*evens, *odds)]
    parts = product([x for row in moved_distant for x in row], weight, labels, plan, types[: len(remote)])
    theirs_even, theirs_odd = parts[: len(evens)], parts[len(evens) :]
    met_theirs = [over_next(x) for x in theirs_odd]

    def onward(even, arrived):
        return [over_slab((x + y.astype(F32)).astype(BF16), m) for x, y, m in zip(even, arrived, evens)]

    terms_ours += onward(ours_even, met)
    met_theirs, late = lax.optimization_barrier((met_theirs, late))
    terms_theirs = onward(theirs_even, met_theirs)
    terms_theirs += [over_slab(x, m) for x, m in zip(late, near[1::2])]
    new_first, new_second = moments(arrays[:3], bulk, first_rows - bulk, made)
    new_first, new_second, terms_near, terms_ours, terms_theirs = lax.optimization_barrier(
        (new_first, new_second, terms_near, terms_ours, terms_theirs)
    )

    def added(terms):
        return sum(x.astype(F32) for x in terms).reshape(-1, PAIR, height, weight.shape[1])

    total = added(terms_near) + jnp.concatenate([added(terms_ours), added(terms_theirs)], axis=0)
    keep = jnp.where(core == 0, total[:, 0], total[:, 1])
    give = jnp.where(core == 0, total[:, 1], total[:, 0])
    results = (keep + over_core(give) + bias).astype(BF16)
    if heads == 2:
        ordered = jnp.where(mine == 0, results, results[::-1])
    else:
        ordered = jnp.take(results, jnp.arange(heads) ^ mine, axis=0)
    projected = ordered.reshape(-1, results.shape[-1])
    return (new_first, new_second, projected)


def solution(mesh):
    rows = P(("dp", "tensor"), None)
    return jax.shard_map(
        on_device,
        mesh=mesh,
        in_specs=(rows, P(), P(None, "tensor"), P("tensor"), rows, rows, rows, rows, rows),
        out_specs=(rows, rows, P("dp", "tensor")),
        check_vma=False,
    )
```

```python
import functools

import jax
import jax.numpy as jnp
from jax import lax
from jax.experimental import pallas as pl
from jax.experimental.pallas import tpu as pltpu
from jax.sharding import PartitionSpec as P

PAIR = 2
CLIP = 448.0
MIB = 1024 * 1024
F32 = jnp.float32
BF16 = jnp.bfloat16
FAR = pl.BlockSpec(memory_space=pltpu.HBM)
NEAR = pl.BlockSpec(memory_space=pltpu.VMEM)
FREE = pl.CostEstimate(flops=0, bytes_accessed=0, transcendentals=0)


def far(x):
    return pltpu.with_memory_space_constraint(x, pltpu.HBM)


def near_by(x):
    return pltpu.with_memory_space_constraint(x, pltpu.VMEM)


def like(shape, dtype):
    return jax.ShapeDtypeStruct(shape, dtype)


def apart(m, core):
    return (m // 2) * 4 + core * 2 + m % 2


def norm_kernel(ours_ref, theirs_ref, gain_ref, *piece_refs):
    dp = lax.axis_index("dp")
    slab, core = dp // PAIR, dp % PAIR
    height = ours_ref.shape[0]
    width = piece_refs[0].shape[1]
    for turn, ref in enumerate((ours_ref, theirs_ref)):
        values = ref[...].astype(F32)
        scale = lax.rsqrt(jnp.mean(values * values, axis=1, keepdims=True) + 1e-06)
        rows = pl.ds(pl.multiple_of((core ^ turn) * height, height), height)
        for m, piece_ref in enumerate(piece_refs):
            columns = pl.ds(pl.multiple_of((slab ^ apart(m, core)) * width, width), width)
            piece_ref[rows, :] = (ref[:, columns].astype(F32) * scale * gain_ref[:, columns]).astype(BF16)


def norm(ours, theirs, gain, slabs):
    height, features = ours.shape
    return pl.pallas_call(
        norm_kernel,
        out_shape=[like((PAIR * height, features // slabs), BF16)] * (slabs // PAIR),
        compiler_params=pltpu.CompilerParams(vmem_limit_bytes=8 * MIB),
        cost_estimate=FREE,
    )(*[near_by(x) for x in (ours, theirs, gain.reshape(1, features))])


def step(first, second, grad):
    return 0.9 * first + 0.1 * grad, 0.95 * second + 0.05 * grad * grad


def delta_kernel(chunks, qrows, qcol, heads, start, count, *refs):
    expo_far, *inputs = refs[:5]
    delta_outs, (b0, b1, b2, b3, expo_ref, sems, expo_sem) = refs[5 : 5 + count], refs[5 + count :]
    bufs = (b0, b1, b2, b3)
    mine = lax.axis_index("tensor")
    rows = inputs[0].shape[0]
    cols = inputs[0].shape[1] // heads
    groups = cols // qcol
    high = rows // chunks
    fetch_expo = pltpu.make_async_copy(expo_far, expo_ref, expo_sem)
    fetch_expo.start()
    turns = [(j, c) for j in range(count) for c in range(chunks)]
    fetches = []
    for n, (j, c) in enumerate(turns):
        here = (j, pl.ds(c * high, high), slice(None))
        at = pl.ds(c * high, high), pl.ds(pl.multiple_of((mine ^ (start + j)) * cols, cols), cols)
        fetches.append([pltpu.make_async_copy(inputs[a].at[at], bufs[a].at[here], sems.at[n, a]) for a in range(4)])
        for f in fetches[-1]:
            f.start()
    fetch_expo.wait()
    for n, (j, c) in enumerate(turns):
        for f in fetches[n]:
            f.wait()
        for b in range(high // qrows):
            row = c * (high // qrows) + b
            here = pl.ds(row * qrows, qrows)
            for g in range(groups):
                lanes = pl.ds(g * qcol, qcol)
                new_first, new_second = step(b0[j, here, lanes], b1[j, here, lanes], b2[j, here, lanes])
                bottom = new_second * lax.rsqrt(new_second) + 1e-08
                inverse = pl.reciprocal(bottom, approx=True)
                inverse = inverse * (2.0 - bottom * inverse)
                corrected = 0.02 * new_first * inverse + b3[j, here, lanes]
                expo = jnp.full((1, qcol), expo_ref[row, (mine ^ (start + j)) * groups + g], jnp.int32).astype(F32)
                most = CLIP * jnp.exp2(-expo)
                delta_outs[j][here, lanes] = jnp.clip(corrected, -most, most).astype(BF16)


def delta(arrays, exponent, heads, start, count, chunks=2):
    rows, full = arrays[0].shape
    qrows, qcol = rows // exponent.shape[0], full // exponent.shape[1]
    cols = full // heads
    chunks = min(chunks, rows // qrows)
    return pl.pallas_call(
        functools.partial(delta_kernel, chunks, qrows, qcol, heads, start, count),
        in_specs=[FAR] * 5,
        out_specs=[NEAR] * count,
        out_shape=[like((rows, cols), BF16)] * count,
        scratch_shapes=[pltpu.VMEM((count, rows, cols), F32)] * 4
        + [
            pltpu.SMEM(exponent.shape, jnp.int32),
            pltpu.SemaphoreType.DMA((count * chunks, 4)),
            pltpu.SemaphoreType.DMA(()),
        ],
        compiler_params=pltpu.CompilerParams(vmem_limit_bytes=16 * MIB),
        cost_estimate=FREE,
    )(*[far(x) for x in (exponent, *arrays)])


def moments_kernel(start, size, chunks, *refs):
    inputs, outs, bufs, sems = refs[:3], refs[-8:-6], refs[-6:-1], refs[-1]
    high = size // chunks
    turns = [(pl.ds(start + c * high, high), pl.ds(c * high, high)) for c in range(chunks)]
    fetches = [
        [pltpu.make_async_copy(inputs[a].at[there], bufs[a].at[here], sems.at[c, a]) for a in range(3)]
        for c, (there, here) in enumerate(turns)
    ]
    stores = [
        [pltpu.make_async_copy(bufs[3 + a].at[here], outs[a].at[there], sems.at[c, 3 + a]) for a in range(2)]
        for c, (there, here) in enumerate(turns)
    ]
    for row in fetches:
        for f in row:
            f.start()
    for c, (_, here) in enumerate(turns):
        for f in fetches[c]:
            f.wait()
        bufs[3][here, :], bufs[4][here, :] = step(bufs[0][here, :], bufs[1][here, :], bufs[2][here, :])
        for s in stores[c]:
            s.start()
    for row in stores:
        for s in row:
            s.wait()


def moments(arrays, start, size, made=(), chunks=4):
    rows, full = arrays[0].shape
    chunks = min(chunks, size // 8)
    return pl.pallas_call(
        functools.partial(moments_kernel, start, size, chunks),
        in_specs=[FAR] * (3 + len(made)),
        out_specs=[FAR] * 2,
        out_shape=[like((rows, full), F32)] * 2,
        scratch_shapes=[pltpu.VMEM((size, full), F32)] * 5 + [pltpu.SemaphoreType.DMA((chunks, 5))],
        input_output_aliases={3 + i: i for i in range(len(made))},
        compiler_params=pltpu.CompilerParams(vmem_limit_bytes=16 * MIB),
        cost_estimate=pl.CostEstimate(flops=0, bytes_accessed=60 * rows * full, transcendentals=0),
    )(*[far(x) for x in (*arrays, *made)])


def multiply(piece_refs, labels, weight, plan, out_refs):
    stacked = jnp.concatenate([r[...] for r in piece_refs], axis=0)
    total = jnp.dot(stacked, weight, preferred_element_type=F32)
    tall = total.shape[0] // len(labels)
    for wanted, out_ref in zip(plan, out_refs):
        for n, label in enumerate(wanted):
            at = labels.index(label) * tall
            out_ref[n * tall : (n + 1) * tall, :] = total[at : at + tall].astype(out_ref.dtype)


def joined(tall, cols, plan, types):
    return [like((len(wanted) * tall, cols), t) for wanted, t in zip(plan, types)]


def places(heads, rows):
    core, mine = lax.axis_index("dp") % PAIR, lax.axis_index("tensor")
    for n in range(PAIR * heads):
        yield ((core ^ (n // heads)) * heads + (mine ^ (n % heads))) * rows


def fetch_kernel(heads, stale_far, out_ref, sems):
    blocks, rows = out_ref.shape[:2]
    copies = []
    for n, at in enumerate(places(heads, rows)):
        first = (lax.axis_index("dp") // PAIR) * (blocks * rows) + at
        source = stale_far.at[pl.ds(pl.multiple_of(first, rows), rows), :]
        copies.append(pltpu.make_async_copy(source, out_ref.at[n], sems.at[n]))
        copies[-1].start()
    for copy in copies:
        copy.wait()


def fetch(stale, heads, slabs):
    blocks = PAIR * heads
    return pl.pallas_call(
        functools.partial(fetch_kernel, heads),
        in_specs=[FAR],
        out_specs=NEAR,
        out_shape=like((blocks, stale.shape[0] // slabs // blocks, stale.shape[1]), BF16),
        scratch_shapes=[pltpu.SemaphoreType.DMA((blocks,))],
        compiler_params=pltpu.CompilerParams(vmem_limit_bytes=8 * MIB),
        cost_estimate=FREE,
    )(far(stale))


def merge_kernel(heads, labels, plan, stale_ref, *refs):
    blocks = PAIR * heads
    delta_refs, piece_refs = refs[:blocks], refs[blocks : -(len(plan) + 1)]
    weight_ref, *out_refs = refs[-(len(plan) + 1) :]
    rows = delta_refs[0].shape[0]
    for n, at in enumerate(places(heads, rows)):
        here = pl.ds(pl.multiple_of(at, rows), rows)
        weight_ref[here, :] = (stale_ref[n].astype(F32) + delta_refs[n][...].astype(F32)).astype(BF16)
    multiply(piece_refs, labels, weight_ref[...], plan, out_refs)


def product_kernel(labels, plan, *refs):
    *piece_refs, weight_ref = refs[: -len(plan)]
    multiply(piece_refs, labels, weight_ref[...], plan, refs[-len(plan) :])


def merge_product(stale, deltas, pieces, heads, labels, plan, types):
    rows, cols = deltas[0].shape
    blocks = len(deltas)
    tall = sum(p.shape[0] for p in pieces) // len(labels)
    return pl.pallas_call(
        functools.partial(merge_kernel, heads, labels, plan),
        out_shape=[like((blocks * rows, cols), BF16)] + joined(tall, cols, plan, types),
        compiler_params=pltpu.CompilerParams(vmem_limit_bytes=16 * MIB),
        cost_estimate=pl.CostEstimate(flops=0, bytes_accessed=8 * blocks * rows * cols, transcendentals=0),
    )(*[near_by(x) for x in (stale, *deltas, *pieces)])


def product(pieces, weight, labels, plan, types):
    tall = sum(p.shape[0] for p in pieces) // len(labels)
    return pl.pallas_call(
        functools.partial(product_kernel, labels, plan),
        out_shape=joined(tall, weight.shape[1], plan, types),
        compiler_params=pltpu.CompilerParams(vmem_limit_bytes=12 * MIB),
        cost_estimate=FREE,
    )(*[near_by(x) for x in (*pieces, weight)])


def on_device(tokens, gain, stale, bias, first, second, grad, residual, exponent):
    heads = lax.axis_size("tensor")
    replicas = lax.axis_size("dp")
    slabs = replicas // PAIR
    partners = slabs // PAIR
    near, remote = range(partners // 2), range(partners // 2, partners)
    core, mine = lax.axis_index("dp") % PAIR, lax.axis_index("tensor")
    height = tokens.shape[0]

    def over_tensor(x, j):
        return x if j == 0 else lax.ppermute(x, "tensor", [(i, i ^ j) for i in range(heads)])

    def over_core(x):
        return lax.ppermute(x, "dp", [(i, i ^ 1) for i in range(replicas)])

    def over_slab(x, m):
        pairs = [(i, ((i // PAIR) ^ apart(m, i % PAIR)) * PAIR + i % PAIR) for i in range(replicas)]
        return lax.ppermute(x, "dp", pairs)

    def over_next(x):
        return lax.ppermute(x, "dp", [(i, i ^ PAIR) for i in range(replicas)])

    beside = over_core(tokens)
    arrays = (first, second, grad, residual)
    theirs = delta(arrays, exponent, heads, 1, heads - 1)
    theirs, beside = lax.optimization_barrier((theirs, beside))
    arrived = [over_tensor(theirs[j], j + 1) for j in range(heads - 1)]
    normed = norm(tokens, beside, gain, slabs)
    order = (*remote, *near)
    pieces = [over_slab(normed[m], m) for m in order]
    exponent, normed = lax.optimization_barrier((exponent, normed))
    ours = delta(arrays, exponent, heads, 0, 1)
    distant, close = pieces[: len(remote)], pieces[len(remote) :]

    def over_heads(group):
        return [[over_tensor(x, j) for x in group] for j in range(1, heads)]

    ours, close = lax.optimization_barrier((ours, close))
    moved_close = over_heads(close)
    first_rows = first.shape[0]
    bulk = first_rows // 2
    made = moments(arrays[:3], 0, bulk)
    held = fetch(stale, heads, slabs)
    made, held, distant, arrived, moved_close = lax.optimization_barrier((made, held, distant, arrived, moved_close))
    moved_distant = over_heads([jnp.concatenate(distant, axis=0)])
    shared = [*ours, *arrived]
    shared = shared + [over_core(x) for x in shared]
    peers = range(1, heads)
    evens, odds = remote[::2], remote[1::2]
    labels = [(0, m) for m in remote]
    plan = [[(0, m)] for m in (*evens, *odds)]
    types = [F32] * len(evens) + [BF16] * len(odds)
    weight, *parts = merge_product(held, shared, distant, heads, labels, plan, types)
    ours_even, ours_odd = parts[: len(evens)], parts[len(evens) :]
    met = [over_next(x) for x in ours_odd]
    labels = [(j, m) for j in range(heads) for m in near]
    plan = [[(j, m) for j in range(heads)] for m in near[::2]]
    plan += [[(j, m) for j in group] for group in ([0], peers) for m in near[1::2]]
    blocks = [*close, *[x for row in moved_close for x in row]]
    parts_near = product(blocks, weight, labels, plan, [BF16] * len(plan))
    split = len(near[::2])
    last = split + len(near[1::2])
    terms_near = [over_slab(x, m) for x, m in zip(parts_near[:split], near[::2])]
    late = parts_near[split:]
    met, moved_distant = lax.optimization_barrier((met, moved_distant))

    labels = [(j, m) for j in peers for m in remote]
    plan = [[(j, m) for j in peers] for m in (*evens, *odds)]
    parts = product([x for row in moved_distant for x in row], weight, labels, plan, types[: len(remote)])
    theirs_even, theirs_odd = parts[: len(evens)], parts[len(evens) :]
    met_theirs = [over_next(x) for x in theirs_odd]

    def onward(even, arrived):
        return [over_slab((x + y.astype(F32)).astype(BF16), m) for x, y, m in zip(even, arrived, evens)]

    terms_ours = onward(ours_even, met)
    met_theirs, late = lax.optimization_barrier((met_theirs, late))
    terms_theirs = onward(theirs_even, met_theirs)
    terms_theirs += [over_slab(x, m) for x, m in zip(late[last - split :], near[1::2])]
    terms_ours += [over_slab(x, m) for x, m in zip(late, near[1::2])]
    new_first, new_second = moments(arrays[:3], bulk, first_rows - bulk, made)
    new_first, new_second, terms_near, terms_ours, terms_theirs = lax.optimization_barrier(
        (new_first, new_second, terms_near, terms_ours, terms_theirs)
    )

    def added(terms):
        return sum(x.astype(F32) for x in terms).reshape(-1, PAIR, height, weight.shape[1])

    total = added(terms_near) + jnp.concatenate([added(terms_ours), added(terms_theirs)], axis=0)
    keep = jnp.where(core == 0, total[:, 0], total[:, 1])
    give = jnp.where(core == 0, total[:, 1], total[:, 0])
    results = (keep + over_core(give.astype(BF16)).astype(F32) + bias).astype(BF16)
    if heads == 2:
        ordered = jnp.where(mine == 0, results, results[::-1])
    else:
        ordered = jnp.take(results, jnp.arange(heads) ^ mine, axis=0)
    projected = ordered.reshape(-1, results.shape[-1])
    return (new_first, new_second, projected)


def solution(mesh):
    rows = P(("dp", "tensor"), None)
    return jax.shard_map(
        on_device,
        mesh=mesh,
        in_specs=(rows, P(), P(None, "tensor"), P("tensor"), rows, rows, rows, rows, rows),
        out_specs=(rows, rows, P("dp", "tensor")),
        check_vma=False,
    )
```

```python
import functools

import jax
import jax.numpy as jnp
from jax import lax
from jax.experimental import pallas as pl
from jax.experimental.pallas import tpu as pltpu
from jax.sharding import PartitionSpec as P

PAIR = 2
CLIP = 448.0
MIB = 1024 * 1024
F32 = jnp.float32
BF16 = jnp.bfloat16
FAR = pl.BlockSpec(memory_space=pltpu.HBM)
NEAR = pl.BlockSpec(memory_space=pltpu.VMEM)
FREE = pl.CostEstimate(flops=0, bytes_accessed=0, transcendentals=0)


def far(x):
    return pltpu.with_memory_space_constraint(x, pltpu.HBM)


def near_by(x):
    return pltpu.with_memory_space_constraint(x, pltpu.VMEM)


def like(shape, dtype):
    return jax.ShapeDtypeStruct(shape, dtype)


def apart(m, core):
    return (m // 2) * 4 + core * 2 + m % 2


def norm_kernel(ours_ref, theirs_ref, gain_ref, *piece_refs):
    dp = lax.axis_index("dp")
    slab, core = dp // PAIR, dp % PAIR
    height = ours_ref.shape[0]
    width = piece_refs[0].shape[1]
    for turn, ref in enumerate((ours_ref, theirs_ref)):
        values = ref[...].astype(F32)
        scale = lax.rsqrt(jnp.mean(values * values, axis=1, keepdims=True) + 1e-06)
        rows = pl.ds(pl.multiple_of((core ^ turn) * height, height), height)
        for m, piece_ref in enumerate(piece_refs):
            columns = pl.ds(pl.multiple_of((slab ^ apart(m, core)) * width, width), width)
            piece_ref[rows, :] = (ref[:, columns].astype(F32) * scale * gain_ref[:, columns]).astype(BF16)


def norm(ours, theirs, gain, slabs):
    height, features = ours.shape
    return pl.pallas_call(
        norm_kernel,
        out_shape=[like((PAIR * height, features // slabs), BF16)] * (slabs // PAIR),
        compiler_params=pltpu.CompilerParams(vmem_limit_bytes=8 * MIB),
        cost_estimate=FREE,
    )(*[near_by(x) for x in (ours, theirs, gain.reshape(1, features))])


def step(first, second, grad):
    return 0.9 * first + 0.1 * grad, 0.95 * second + 0.05 * grad * grad


def delta_kernel(chunks, qrows, qcol, heads, start, count, *refs):
    expo_far, *inputs = refs[:5]
    delta_outs, (b0, b1, b2, b3, expo_ref, sems, expo_sem) = refs[5 : 5 + count], refs[5 + count :]
    bufs = (b0, b1, b2, b3)
    mine = lax.axis_index("tensor")
    rows = inputs[0].shape[0]
    cols = inputs[0].shape[1] // heads
    groups = cols // qcol
    high = rows // chunks
    fetch_expo = pltpu.make_async_copy(expo_far, expo_ref, expo_sem)
    fetch_expo.start()
    turns = [(j, c) for j in range(count) for c in range(chunks)]
    fetches = []
    for n, (j, c) in enumerate(turns):
        here = (j, pl.ds(c * high, high), slice(None))
        at = pl.ds(c * high, high), pl.ds(pl.multiple_of((mine ^ (start + j)) * cols, cols), cols)
        fetches.append([pltpu.make_async_copy(inputs[a].at[at], bufs[a].at[here], sems.at[n, a]) for a in range(4)])
        for f in fetches[-1]:
            f.start()
    fetch_expo.wait()
    for n, (j, c) in enumerate(turns):
        for f in fetches[n]:
            f.wait()
        for b in range(high // qrows):
            row = c * (high // qrows) + b
            here = pl.ds(row * qrows, qrows)
            for g in range(groups):
                lanes = pl.ds(g * qcol, qcol)
                new_first, new_second = step(b0[j, here, lanes], b1[j, here, lanes], b2[j, here, lanes])
                bottom = new_second * lax.rsqrt(new_second) + 1e-08
                inverse = pl.reciprocal(bottom, approx=True)
                inverse = inverse * (2.0 - bottom * inverse)
                corrected = 0.02 * new_first * inverse + b3[j, here, lanes]
                expo = jnp.full((1, qcol), expo_ref[row, (mine ^ (start + j)) * groups + g], jnp.int32).astype(F32)
                most = CLIP * jnp.exp2(-expo)
                delta_outs[j][here, lanes] = jnp.clip(corrected, -most, most).astype(BF16)


def delta(arrays, exponent, heads, start, count, chunks=2):
    rows, full = arrays[0].shape
    qrows, qcol = rows // exponent.shape[0], full // exponent.shape[1]
    cols = full // heads
    chunks = min(chunks, rows // qrows)
    return pl.pallas_call(
        functools.partial(delta_kernel, chunks, qrows, qcol, heads, start, count),
        in_specs=[FAR] * 5,
        out_specs=[NEAR] * count,
        out_shape=[like((rows, cols), BF16)] * count,
        scratch_shapes=[pltpu.VMEM((count, rows, cols), F32)] * 4
        + [
            pltpu.SMEM(exponent.shape, jnp.int32),
            pltpu.SemaphoreType.DMA((count * chunks, 4)),
            pltpu.SemaphoreType.DMA(()),
        ],
        compiler_params=pltpu.CompilerParams(vmem_limit_bytes=16 * MIB),
        cost_estimate=FREE,
    )(*[far(x) for x in (exponent, *arrays)])


def moments_kernel(start, size, chunks, *refs):
    inputs, outs, bufs, sems = refs[:3], refs[-8:-6], refs[-6:-1], refs[-1]
    high = size // chunks
    turns = [(pl.ds(start + c * high, high), pl.ds(c * high, high)) for c in range(chunks)]
    fetches = [
        [pltpu.make_async_copy(inputs[a].at[there], bufs[a].at[here], sems.at[c, a]) for a in range(3)]
        for c, (there, here) in enumerate(turns)
    ]
    stores = [
        [pltpu.make_async_copy(bufs[3 + a].at[here], outs[a].at[there], sems.at[c, 3 + a]) for a in range(2)]
        for c, (there, here) in enumerate(turns)
    ]
    for row in fetches:
        for f in row:
            f.start()
    for c, (_, here) in enumerate(turns):
        for f in fetches[c]:
            f.wait()
        bufs[3][here, :], bufs[4][here, :] = step(bufs[0][here, :], bufs[1][here, :], bufs[2][here, :])
        for s in stores[c]:
            s.start()
    for row in stores:
        for s in row:
            s.wait()


def moments(arrays, start, size, made=(), chunks=4):
    rows, full = arrays[0].shape
    chunks = min(chunks, size // 8)
    return pl.pallas_call(
        functools.partial(moments_kernel, start, size, chunks),
        in_specs=[FAR] * (3 + len(made)),
        out_specs=[FAR] * 2,
        out_shape=[like((rows, full), F32)] * 2,
        scratch_shapes=[pltpu.VMEM((size, full), F32)] * 5 + [pltpu.SemaphoreType.DMA((chunks, 5))],
        input_output_aliases={3 + i: i for i in range(len(made))},
        compiler_params=pltpu.CompilerParams(vmem_limit_bytes=16 * MIB),
        cost_estimate=pl.CostEstimate(flops=0, bytes_accessed=60 * rows * full, transcendentals=0),
    )(*[far(x) for x in (*arrays, *made)])


def multiply(piece_refs, labels, weight, plan, out_refs):
    stacked = jnp.concatenate([r[...] for r in piece_refs], axis=0)
    total = jnp.dot(stacked, weight, preferred_element_type=F32)
    tall = total.shape[0] // len(labels)
    for wanted, out_ref in zip(plan, out_refs):
        for n, label in enumerate(wanted):
            at = labels.index(label) * tall
            out_ref[n * tall : (n + 1) * tall, :] = total[at : at + tall].astype(out_ref.dtype)


def joined(tall, cols, plan, types):
    return [like((len(wanted) * tall, cols), t) for wanted, t in zip(plan, types)]


def places(heads, rows):
    core, mine = lax.axis_index("dp") % PAIR, lax.axis_index("tensor")
    for n in range(PAIR * heads):
        yield ((core ^ (n // heads)) * heads + (mine ^ (n % heads))) * rows


def fetch_kernel(heads, stale_far, out_ref, sems):
    blocks, rows = out_ref.shape[:2]
    copies = []
    for n, at in enumerate(places(heads, rows)):
        first = (lax.axis_index("dp") // PAIR) * (blocks * rows) + at
        source = stale_far.at[pl.ds(pl.multiple_of(first, rows), rows), :]
        copies.append(pltpu.make_async_copy(source, out_ref.at[n], sems.at[n]))
        copies[-1].start()
    for copy in copies:
        copy.wait()


def fetch(stale, heads, slabs):
    blocks = PAIR * heads
    return pl.pallas_call(
        functools.partial(fetch_kernel, heads),
        in_specs=[FAR],
        out_specs=NEAR,
        out_shape=like((blocks, stale.shape[0] // slabs // blocks, stale.shape[1]), BF16),
        scratch_shapes=[pltpu.SemaphoreType.DMA((blocks,))],
        compiler_params=pltpu.CompilerParams(vmem_limit_bytes=8 * MIB),
        cost_estimate=FREE,
    )(far(stale))


def merge_kernel(heads, labels, plan, stale_ref, *refs):
    blocks = PAIR * heads
    delta_refs, piece_refs = refs[:blocks], refs[blocks : -(len(plan) + 1)]
    weight_ref, *out_refs = refs[-(len(plan) + 1) :]
    rows = delta_refs[0].shape[0]
    for n, at in enumerate(places(heads, rows)):
        here = pl.ds(pl.multiple_of(at, rows), rows)
        weight_ref[here, :] = (stale_ref[n].astype(F32) + delta_refs[n][...].astype(F32)).astype(BF16)
    multiply(piece_refs, labels, weight_ref[...], plan, out_refs)


def product_kernel(labels, plan, *refs):
    *piece_refs, weight_ref = refs[: -len(plan)]
    multiply(piece_refs, labels, weight_ref[...], plan, refs[-len(plan) :])


def merge_product(stale, deltas, pieces, heads, labels, plan, types):
    rows, cols = deltas[0].shape
    blocks = len(deltas)
    tall = sum(p.shape[0] for p in pieces) // len(labels)
    return pl.pallas_call(
        functools.partial(merge_kernel, heads, labels, plan),
        out_shape=[like((blocks * rows, cols), BF16)] + joined(tall, cols, plan, types),
        compiler_params=pltpu.CompilerParams(vmem_limit_bytes=16 * MIB),
        cost_estimate=pl.CostEstimate(flops=0, bytes_accessed=8 * blocks * rows * cols, transcendentals=0),
    )(*[near_by(x) for x in (stale, *deltas, *pieces)])


def product(pieces, weight, labels, plan, types):
    tall = sum(p.shape[0] for p in pieces) // len(labels)
    return pl.pallas_call(
        functools.partial(product_kernel, labels, plan),
        out_shape=joined(tall, weight.shape[1], plan, types),
        compiler_params=pltpu.CompilerParams(vmem_limit_bytes=12 * MIB),
        cost_estimate=FREE,
    )(*[near_by(x) for x in (*pieces, weight)])


def on_device(tokens, gain, stale, bias, first, second, grad, residual, exponent):
    heads = lax.axis_size("tensor")
    replicas = lax.axis_size("dp")
    slabs = replicas // PAIR
    partners = slabs // PAIR
    near, remote = range(partners // 2), range(partners // 2, partners)
    core, mine = lax.axis_index("dp") % PAIR, lax.axis_index("tensor")
    height = tokens.shape[0]

    def over_tensor(x, j):
        return x if j == 0 else lax.ppermute(x, "tensor", [(i, i ^ j) for i in range(heads)])

    def over_core(x):
        return lax.ppermute(x, "dp", [(i, i ^ 1) for i in range(replicas)])

    def over_slab(x, m):
        pairs = [(i, ((i // PAIR) ^ apart(m, i % PAIR)) * PAIR + i % PAIR) for i in range(replicas)]
        return lax.ppermute(x, "dp", pairs)

    def over_next(x):
        return lax.ppermute(x, "dp", [(i, i ^ PAIR) for i in range(replicas)])

    beside = over_core(tokens)
    arrays = (first, second, grad, residual)
    theirs = delta(arrays, exponent, heads, 1, heads - 1)
    theirs, beside = lax.optimization_barrier((theirs, beside))
    arrived = [over_tensor(theirs[j], j + 1) for j in range(heads - 1)]
    normed = norm(tokens, beside, gain, slabs)
    order = (*remote, *near)
    pieces = [over_slab(normed[m], m) for m in order]
    exponent, normed = lax.optimization_barrier((exponent, normed))
    ours = delta(arrays, exponent, heads, 0, 1)
    distant, close = pieces[: len(remote)], pieces[len(remote) :]

    def over_heads(group):
        return [[over_tensor(x, j) for x in group] for j in range(1, heads)]

    ours, close = lax.optimization_barrier((ours, close))
    moved_close = over_heads(close)
    first_rows = first.shape[0]
    bulk = first_rows // 2
    made = moments(arrays[:3], 0, bulk)
    held = fetch(stale, heads, slabs)
    made, held, distant, arrived, moved_close = lax.optimization_barrier((made, held, distant, arrived, moved_close))
    moved_distant = over_heads([jnp.concatenate(distant, axis=0)])
    shared = [*ours, *arrived]
    shared = shared + [over_core(x) for x in shared]
    peers = range(1, heads)
    evens, odds = remote[::2], remote[1::2]
    labels = [(0, m) for m in remote]
    plan = [[(0, m)] for m in (*evens, *odds)]
    types = [F32] * len(evens) + [BF16] * len(odds)
    weight, *parts = merge_product(held, shared, distant, heads, labels, plan, types)
    ours_even, ours_odd = parts[: len(evens)], parts[len(evens) :]
    met = [over_next(x) for x in ours_odd]
    labels = [(j, m) for j in range(heads) for m in near]
    plan = [[(j, m) for j in range(heads)] for m in near[::2]]
    plan += [[(j, m) for j in group] for group in ([0], peers) for m in near[1::2]]
    blocks = [*close, *[x for row in moved_close for x in row]]
    parts_near = product(blocks, weight, labels, plan, [BF16] * len(plan))
    split = len(near[::2])
    last = split + len(near[1::2])
    terms_near = [over_slab(x, m) for x, m in zip(parts_near[:split], near[::2])]
    middle, late = parts_near[split:last], parts_near[last:]
    met, moved_distant = lax.optimization_barrier((met, moved_distant))

    labels = [(j, m) for j in peers for m in remote]
    plan = [[(j, m) for j in peers] for m in (*evens, *odds)]
    parts = product([x for row in moved_distant for x in row], weight, labels, plan, types[: len(remote)])
    theirs_even, theirs_odd = parts[: len(evens)], parts[len(evens) :]
    theirs_odd, middle = lax.optimization_barrier((theirs_odd, middle))
    met_theirs = [over_next(x) for x in theirs_odd]

    def onward(even, arrived):
        return [over_slab((x + y.astype(F32)).astype(BF16), m) for x, y, m in zip(even, arrived, evens)]

    terms_ours = [over_slab(x, m) for x, m in zip(middle, near[1::2])]
    terms_ours += onward(ours_even, met)
    met_theirs, late = lax.optimization_barrier((met_theirs, late))
    terms_theirs = onward(theirs_even, met_theirs)
    terms_theirs += [over_slab(x, m) for x, m in zip(late, near[1::2])]
    new_first, new_second = moments(arrays[:3], bulk, first_rows - bulk, made)
    new_first, new_second, terms_near, terms_ours, terms_theirs = lax.optimization_barrier(
        (new_first, new_second, terms_near, terms_ours, terms_theirs)
    )

    def added(terms):
        return sum(x.astype(F32) for x in terms).reshape(-1, PAIR, height, weight.shape[1])

    total = added(terms_near) + jnp.concatenate([added(terms_ours), added(terms_theirs)], axis=0)
    keep = jnp.where(core == 0, total[:, 0], total[:, 1])
    give = jnp.where(core == 0, total[:, 1], total[:, 0])
    results = (keep + over_core(give.astype(BF16)).astype(F32) + bias).astype(BF16)
    if heads == 2:
        ordered = jnp.where(mine == 0, results, results[::-1])
    else:
        ordered = jnp.take(results, jnp.arange(heads) ^ mine, axis=0)
    projected = ordered.reshape(-1, results.shape[-1])
    return (new_first, new_second, projected)


def solution(mesh):
    rows = P(("dp", "tensor"), None)
    return jax.shard_map(
        on_device,
        mesh=mesh,
        in_specs=(rows, P(), P(None, "tensor"), P("tensor"), rows, rows, rows, rows, rows),
        out_specs=(rows, rows, P("dp", "tensor")),
        check_vma=False,
    )
```

```python
import functools

import jax
import jax.numpy as jnp
from jax import lax
from jax.experimental import pallas as pl
from jax.experimental.pallas import tpu as pltpu
from jax.sharding import PartitionSpec as P

PAIR = 2
CLIP = 448.0
MIB = 1024 * 1024
F32 = jnp.float32
BF16 = jnp.bfloat16
FAR = pl.BlockSpec(memory_space=pltpu.HBM)
NEAR = pl.BlockSpec(memory_space=pltpu.VMEM)
FREE = pl.CostEstimate(flops=0, bytes_accessed=0, transcendentals=0)


def far(x):
    return pltpu.with_memory_space_constraint(x, pltpu.HBM)


def near_by(x):
    return pltpu.with_memory_space_constraint(x, pltpu.VMEM)


def like(shape, dtype):
    return jax.ShapeDtypeStruct(shape, dtype)


def apart(m, core):
    return (m // 2) * 4 + core * 2 + m % 2


def norm_kernel(ours_ref, theirs_ref, gain_ref, *piece_refs):
    dp = lax.axis_index("dp")
    slab, core = dp // PAIR, dp % PAIR
    height = ours_ref.shape[0]
    width = piece_refs[0].shape[1]
    for turn, ref in enumerate((ours_ref, theirs_ref)):
        values = ref[...].astype(F32)
        scale = lax.rsqrt(jnp.mean(values * values, axis=1, keepdims=True) + 1e-06)
        rows = pl.ds(pl.multiple_of((core ^ turn) * height, height), height)
        for m, piece_ref in enumerate(piece_refs):
            columns = pl.ds(pl.multiple_of((slab ^ apart(m, core)) * width, width), width)
            piece_ref[rows, :] = (ref[:, columns].astype(F32) * scale * gain_ref[:, columns]).astype(BF16)


def norm(ours, theirs, gain, slabs):
    height, features = ours.shape
    return pl.pallas_call(
        norm_kernel,
        out_shape=[like((PAIR * height, features // slabs), BF16)] * (slabs // PAIR),
        compiler_params=pltpu.CompilerParams(vmem_limit_bytes=8 * MIB),
        cost_estimate=FREE,
    )(*[near_by(x) for x in (ours, theirs, gain.reshape(1, features))])


def step(first, second, grad):
    return 0.9 * first + 0.1 * grad, 0.95 * second + 0.05 * grad * grad


def delta_kernel(chunks, qrows, qcol, heads, start, count, *refs):
    expo_far, *inputs = refs[:5]
    delta_outs, (b0, b1, b2, b3, expo_ref, sems, expo_sem) = refs[5 : 5 + count], refs[5 + count :]
    bufs = (b0, b1, b2, b3)
    mine = lax.axis_index("tensor")
    rows = inputs[0].shape[0]
    cols = inputs[0].shape[1] // heads
    groups = cols // qcol
    high = rows // chunks
    fetch_expo = pltpu.make_async_copy(expo_far, expo_ref, expo_sem)
    fetch_expo.start()
    turns = [(j, c) for j in range(count) for c in range(chunks)]
    fetches = []
    for n, (j, c) in enumerate(turns):
        here = (j, pl.ds(c * high, high), slice(None))
        at = pl.ds(c * high, high), pl.ds(pl.multiple_of((mine ^ (start + j)) * cols, cols), cols)
        fetches.append([pltpu.make_async_copy(inputs[a].at[at], bufs[a].at[here], sems.at[n, a]) for a in range(4)])
        for f in fetches[-1]:
            f.start()
    fetch_expo.wait()
    for n, (j, c) in enumerate(turns):
        for f in fetches[n]:
            f.wait()
        for b in range(high // qrows):
            row = c * (high // qrows) + b
            here = pl.ds(row * qrows, qrows)
            for g in range(groups):
                lanes = pl.ds(g * qcol, qcol)
                new_first, new_second = step(b0[j, here, lanes], b1[j, here, lanes], b2[j, here, lanes])
                corrected = 0.02 * new_first / (jnp.sqrt(new_second) + 1e-08) + b3[j, here, lanes]
                expo = jnp.full((1, qcol), expo_ref[row, (mine ^ (start + j)) * groups + g], jnp.int32).astype(F32)
                most = CLIP * jnp.exp2(-expo)
                delta_outs[j][here, lanes] = jnp.clip(corrected, -most, most).astype(BF16)


def delta(arrays, exponent, heads, start, count, chunks=4):
    rows, full = arrays[0].shape
    qrows, qcol = rows // exponent.shape[0], full // exponent.shape[1]
    cols = full // heads
    chunks = min(chunks, rows // qrows)
    return pl.pallas_call(
        functools.partial(delta_kernel, chunks, qrows, qcol, heads, start, count),
        in_specs=[FAR] * 5,
        out_specs=[NEAR] * count,
        out_shape=[like((rows, cols), BF16)] * count,
        scratch_shapes=[pltpu.VMEM((count, rows, cols), F32)] * 4
        + [
            pltpu.SMEM(exponent.shape, jnp.int32),
            pltpu.SemaphoreType.DMA((count * chunks, 4)),
            pltpu.SemaphoreType.DMA(()),
        ],
        compiler_params=pltpu.CompilerParams(vmem_limit_bytes=16 * MIB),
        cost_estimate=FREE,
    )(*[far(x) for x in (exponent, *arrays)])


def moments_kernel(start, size, chunks, *refs):
    inputs, outs, bufs, sems = refs[:3], refs[-8:-6], refs[-6:-1], refs[-1]
    high = size // chunks
    turns = [(pl.ds(start + c * high, high), pl.ds(c * high, high)) for c in range(chunks)]
    fetches = [
        [pltpu.make_async_copy(inputs[a].at[there], bufs[a].at[here], sems.at[c, a]) for a in range(3)]
        for c, (there, here) in enumerate(turns)
    ]
    stores = [
        [pltpu.make_async_copy(bufs[3 + a].at[here], outs[a].at[there], sems.at[c, 3 + a]) for a in range(2)]
        for c, (there, here) in enumerate(turns)
    ]
    for row in fetches:
        for f in row:
            f.start()
    for c, (_, here) in enumerate(turns):
        for f in fetches[c]:
            f.wait()
        bufs[3][here, :], bufs[4][here, :] = step(bufs[0][here, :], bufs[1][here, :], bufs[2][here, :])
        for s in stores[c]:
            s.start()
    for row in stores:
        for s in row:
            s.wait()


def moments(arrays, start, size, made=(), chunks=4):
    rows, full = arrays[0].shape
    chunks = min(chunks, size // 8)
    return pl.pallas_call(
        functools.partial(moments_kernel, start, size, chunks),
        in_specs=[FAR] * (3 + len(made)),
        out_specs=[FAR] * 2,
        out_shape=[like((rows, full), F32)] * 2,
        scratch_shapes=[pltpu.VMEM((size, full), F32)] * 5 + [pltpu.SemaphoreType.DMA((chunks, 5))],
        input_output_aliases={3 + i: i for i in range(len(made))},
        compiler_params=pltpu.CompilerParams(vmem_limit_bytes=16 * MIB),
        cost_estimate=pl.CostEstimate(flops=0, bytes_accessed=60 * rows * full, transcendentals=0),
    )(*[far(x) for x in (*arrays, *made)])


def multiply(piece_refs, labels, weight, plan, out_refs):
    stacked = jnp.concatenate([r[...] for r in piece_refs], axis=0)
    total = jnp.dot(stacked, weight, preferred_element_type=F32)
    tall = total.shape[0] // len(labels)
    for wanted, out_ref in zip(plan, out_refs):
        for n, label in enumerate(wanted):
            at = labels.index(label) * tall
            out_ref[n * tall : (n + 1) * tall, :] = total[at : at + tall].astype(out_ref.dtype)


def joined(tall, cols, plan, types):
    return [like((len(wanted) * tall, cols), t) for wanted, t in zip(plan, types)]


def places(heads, rows):
    core, mine = lax.axis_index("dp") % PAIR, lax.axis_index("tensor")
    for n in range(PAIR * heads):
        yield ((core ^ (n // heads)) * heads + (mine ^ (n % heads))) * rows


def fetch_kernel(heads, stale_far, out_ref, sems):
    blocks, rows = out_ref.shape[:2]
    copies = []
    for n, at in enumerate(places(heads, rows)):
        first = (lax.axis_index("dp") // PAIR) * (blocks * rows) + at
        source = stale_far.at[pl.ds(pl.multiple_of(first, rows), rows), :]
        copies.append(pltpu.make_async_copy(source, out_ref.at[n], sems.at[n]))
        copies[-1].start()
    for copy in copies:
        copy.wait()


def fetch(stale, heads, slabs):
    blocks = PAIR * heads
    return pl.pallas_call(
        functools.partial(fetch_kernel, heads),
        in_specs=[FAR],
        out_specs=NEAR,
        out_shape=like((blocks, stale.shape[0] // slabs // blocks, stale.shape[1]), BF16),
        scratch_shapes=[pltpu.SemaphoreType.DMA((blocks,))],
        compiler_params=pltpu.CompilerParams(vmem_limit_bytes=8 * MIB),
        cost_estimate=FREE,
    )(far(stale))


def merge_kernel(heads, labels, plan, stale_ref, *refs):
    blocks = PAIR * heads
    delta_refs, piece_refs = refs[:blocks], refs[blocks : -(len(plan) + 1)]
    weight_ref, *out_refs = refs[-(len(plan) + 1) :]
    rows = delta_refs[0].shape[0]
    for n, at in enumerate(places(heads, rows)):
        here = pl.ds(pl.multiple_of(at, rows), rows)
        weight_ref[here, :] = (stale_ref[n].astype(F32) + delta_refs[n][...].astype(F32)).astype(BF16)
    multiply(piece_refs, labels, weight_ref[...], plan, out_refs)


def product_kernel(labels, plan, *refs):
    *piece_refs, weight_ref = refs[: -len(plan)]
    multiply(piece_refs, labels, weight_ref[...], plan, refs[-len(plan) :])


def merge_product(stale, deltas, pieces, heads, labels, plan, types):
    rows, cols = deltas[0].shape
    blocks = len(deltas)
    tall = sum(p.shape[0] for p in pieces) // len(labels)
    return pl.pallas_call(
        functools.partial(merge_kernel, heads, labels, plan),
        out_shape=[like((blocks * rows, cols), BF16)] + joined(tall, cols, plan, types),
        compiler_params=pltpu.CompilerParams(vmem_limit_bytes=16 * MIB),
        cost_estimate=pl.CostEstimate(flops=0, bytes_accessed=8 * blocks * rows * cols, transcendentals=0),
    )(*[near_by(x) for x in (stale, *deltas, *pieces)])


def product(pieces, weight, labels, plan, types):
    tall = sum(p.shape[0] for p in pieces) // len(labels)
    return pl.pallas_call(
        functools.partial(product_kernel, labels, plan),
        out_shape=joined(tall, weight.shape[1], plan, types),
        compiler_params=pltpu.CompilerParams(vmem_limit_bytes=12 * MIB),
        cost_estimate=FREE,
    )(*[near_by(x) for x in (*pieces, weight)])


def on_device(tokens, gain, stale, bias, first, second, grad, residual, exponent):
    heads = lax.axis_size("tensor")
    replicas = lax.axis_size("dp")
    slabs = replicas // PAIR
    partners = slabs // PAIR
    near, remote = range(partners // 2), range(partners // 2, partners)
    core, mine = lax.axis_index("dp") % PAIR, lax.axis_index("tensor")
    height = tokens.shape[0]

    def over_tensor(x, j):
        return x if j == 0 else lax.ppermute(x, "tensor", [(i, i ^ j) for i in range(heads)])

    def over_core(x):
        return lax.ppermute(x, "dp", [(i, i ^ 1) for i in range(replicas)])

    def over_slab(x, m):
        pairs = [(i, ((i // PAIR) ^ apart(m, i % PAIR)) * PAIR + i % PAIR) for i in range(replicas)]
        return lax.ppermute(x, "dp", pairs)

    def over_next(x):
        return lax.ppermute(x, "dp", [(i, i ^ PAIR) for i in range(replicas)])

    beside = over_core(tokens)
    arrays = (first, second, grad, residual)
    theirs = delta(arrays, exponent, heads, 1, heads - 1)
    theirs, beside = lax.optimization_barrier((theirs, beside))
    arrived = [over_tensor(theirs[j], j + 1) for j in range(heads - 1)]
    normed = norm(tokens, beside, gain, slabs)
    order = (*remote, *near)
    pieces = [over_slab(normed[m], m) for m in order]
    exponent, normed = lax.optimization_barrier((exponent, normed))
    ours = delta(arrays, exponent, heads, 0, 1)
    distant, close = pieces[: len(remote)], pieces[len(remote) :]

    def over_heads(group):
        return [[over_tensor(x, j) for x in group] for j in range(1, heads)]

    ours, close = lax.optimization_barrier((ours, close))
    moved_close = over_heads(close)
    first_rows = first.shape[0]
    bulk = first_rows * 3 // 4
    made = moments(arrays[:3], 0, bulk)
    held = fetch(stale, heads, slabs)
    made, held, distant, arrived, moved_close = lax.optimization_barrier((made, held, distant, arrived, moved_close))
    moved_distant = over_heads([jnp.concatenate(distant, axis=0)])
    shared = [*ours, *arrived]
    shared = shared + [over_core(x) for x in shared]
    peers = range(1, heads)
    evens, odds = remote[::2], remote[1::2]
    labels = [(0, m) for m in remote]
    plan = [[(0, m)] for m in (*evens, *odds)]
    types = [F32] * len(evens) + [BF16] * len(odds)
    weight, *parts = merge_product(held, shared, distant, heads, labels, plan, types)
    ours_even, ours_odd = parts[: len(evens)], parts[len(evens) :]
    met = [over_next(x) for x in ours_odd]
    labels = [(j, m) for j in range(heads) for m in near]
    plan = [[(j, m) for j in range(heads)] for m in near[::2]]
    plan += [[(j, m) for j in group] for group in ([0], peers) for m in near[1::2]]
    blocks = [*close, *[x for row in moved_close for x in row]]
    parts_near = product(blocks, weight, labels, plan, [BF16] * len(plan))
    split = len(near[::2])
    last = split + len(near[1::2])
    terms_near = [over_slab(x, m) for x, m in zip(parts_near[:split], near[::2])]
    middle, late = parts_near[split:last], parts_near[last:]
    met, moved_distant = lax.optimization_barrier((met, moved_distant))

    labels = [(j, m) for j in peers for m in remote]
    plan = [[(j, m) for j in peers] for m in (*evens, *odds)]
    parts = product([x for row in moved_distant for x in row], weight, labels, plan, types[: len(remote)])
    theirs_even, theirs_odd = parts[: len(evens)], parts[len(evens) :]
    theirs_odd, middle = lax.optimization_barrier((theirs_odd, middle))
    met_theirs = [over_next(x) for x in theirs_odd]

    def onward(even, arrived):
        return [over_slab((x + y.astype(F32)).astype(BF16), m) for x, y, m in zip(even, arrived, evens)]

    terms_ours = [over_slab(x, m) for x, m in zip(middle, near[1::2])]
    terms_ours += onward(ours_even, met)
    met_theirs, late = lax.optimization_barrier((met_theirs, late))
    terms_theirs = onward(theirs_even, met_theirs)
    terms_theirs += [over_slab(x, m) for x, m in zip(late, near[1::2])]
    new_first, new_second = moments(arrays[:3], bulk, first_rows - bulk, made)
    new_first, new_second, terms_near, terms_ours, terms_theirs = lax.optimization_barrier(
        (new_first, new_second, terms_near, terms_ours, terms_theirs)
    )

    def added(terms):
        return sum(x.astype(F32) for x in terms).reshape(-1, PAIR, height, weight.shape[1])

    total = added(terms_near) + jnp.concatenate([added(terms_ours), added(terms_theirs)], axis=0)
    keep = jnp.where(core == 0, total[:, 0], total[:, 1])
    give = jnp.where(core == 0, total[:, 1], total[:, 0])
    results = (keep + over_core(give.astype(BF16)).astype(F32) + bias).astype(BF16)
    if heads == 2:
        ordered = jnp.where(mine == 0, results, results[::-1])
    else:
        ordered = jnp.take(results, jnp.arange(heads) ^ mine, axis=0)
    projected = ordered.reshape(-1, results.shape[-1])
    return (new_first, new_second, projected)


def solution(mesh):
    rows = P(("dp", "tensor"), None)
    return jax.shard_map(
        on_device,
        mesh=mesh,
        in_specs=(rows, P(), P(None, "tensor"), P("tensor"), rows, rows, rows, rows, rows),
        out_specs=(rows, rows, P("dp", "tensor")),
        check_vma=False,
    )
```

```python
import functools

import jax
import jax.numpy as jnp
from jax import lax
from jax.experimental import pallas as pl
from jax.experimental.pallas import tpu as pltpu
from jax.sharding import PartitionSpec as P

PAIR = 2
CLIP = 448.0
MIB = 1024 * 1024
F32 = jnp.float32
BF16 = jnp.bfloat16
FAR = pl.BlockSpec(memory_space=pltpu.HBM)
NEAR = pl.BlockSpec(memory_space=pltpu.VMEM)
FREE = pl.CostEstimate(flops=0, bytes_accessed=0, transcendentals=0)


def far(x):
    return pltpu.with_memory_space_constraint(x, pltpu.HBM)


def near_by(x):
    return pltpu.with_memory_space_constraint(x, pltpu.VMEM)


def like(shape, dtype):
    return jax.ShapeDtypeStruct(shape, dtype)


def apart(m, core):
    return (m // 2) * 4 + core * 2 + m % 2


def norm_kernel(ours_ref, theirs_ref, gain_ref, *piece_refs):
    dp = lax.axis_index("dp")
    slab, core = dp // PAIR, dp % PAIR
    height = ours_ref.shape[0]
    width = piece_refs[0].shape[1]
    for turn, ref in enumerate((ours_ref, theirs_ref)):
        values = ref[...].astype(F32)
        scale = lax.rsqrt(jnp.mean(values * values, axis=1, keepdims=True) + 1e-06)
        rows = pl.ds(pl.multiple_of((core ^ turn) * height, height), height)
        for m, piece_ref in enumerate(piece_refs):
            columns = pl.ds(pl.multiple_of((slab ^ apart(m, core)) * width, width), width)
            piece_ref[rows, :] = (ref[:, columns].astype(F32) * scale * gain_ref[:, columns]).astype(BF16)


def norm(ours, theirs, gain, slabs):
    height, features = ours.shape
    return pl.pallas_call(
        norm_kernel,
        out_shape=[like((PAIR * height, features // slabs), BF16)] * (slabs // PAIR),
        compiler_params=pltpu.CompilerParams(vmem_limit_bytes=8 * MIB),
        cost_estimate=FREE,
    )(*[near_by(x) for x in (ours, theirs, gain.reshape(1, features))])


def step(first, second, grad):
    return 0.9 * first + 0.1 * grad, 0.95 * second + 0.05 * grad * grad


def delta_kernel(chunks, qrows, qcol, heads, start, count, *refs):
    expo_far, *inputs = refs[:5]
    delta_outs, (b0, b1, b2, b3, expo_ref, sems, expo_sem) = refs[5 : 5 + count], refs[5 + count :]
    bufs = (b0, b1, b2, b3)
    mine = lax.axis_index("tensor")
    rows = inputs[0].shape[0]
    cols = inputs[0].shape[1] // heads
    groups = cols // qcol
    high = rows // chunks
    fetch_expo = pltpu.make_async_copy(expo_far, expo_ref, expo_sem)
    fetch_expo.start()
    turns = [(j, c) for j in range(count) for c in range(chunks)]
    fetches = []
    for n, (j, c) in enumerate(turns):
        here = (j, pl.ds(c * high, high), slice(None))
        at = pl.ds(c * high, high), pl.ds(pl.multiple_of((mine ^ (start + j)) * cols, cols), cols)
        fetches.append([pltpu.make_async_copy(inputs[a].at[at], bufs[a].at[here], sems.at[n, a]) for a in range(4)])
        for f in fetches[-1]:
            f.start()
    fetch_expo.wait()
    for n, (j, c) in enumerate(turns):
        for f in fetches[n]:
            f.wait()
        for b in range(high // qrows):
            row = c * (high // qrows) + b
            here = pl.ds(row * qrows, qrows)
            for g in range(groups):
                lanes = pl.ds(g * qcol, qcol)
                new_first, new_second = step(b0[j, here, lanes], b1[j, here, lanes], b2[j, here, lanes])
                corrected = 0.02 * new_first / (jnp.sqrt(new_second) + 1e-08) + b3[j, here, lanes]
                expo = jnp.full((1, qcol), expo_ref[row, (mine ^ (start + j)) * groups + g], jnp.int32).astype(F32)
                most = CLIP * jnp.exp2(-expo)
                delta_outs[j][here, lanes] = jnp.clip(corrected, -most, most).astype(BF16)


def delta(arrays, exponent, heads, start, count, chunks=4):
    rows, full = arrays[0].shape
    qrows, qcol = rows // exponent.shape[0], full // exponent.shape[1]
    cols = full // heads
    chunks = min(chunks, rows // qrows)
    return pl.pallas_call(
        functools.partial(delta_kernel, chunks, qrows, qcol, heads, start, count),
        in_specs=[FAR] * 5,
        out_specs=[NEAR] * count,
        out_shape=[like((rows, cols), BF16)] * count,
        scratch_shapes=[pltpu.VMEM((count, rows, cols), F32)] * 4
        + [
            pltpu.SMEM(exponent.shape, jnp.int32),
            pltpu.SemaphoreType.DMA((count * chunks, 4)),
            pltpu.SemaphoreType.DMA(()),
        ],
        compiler_params=pltpu.CompilerParams(vmem_limit_bytes=16 * MIB),
        cost_estimate=FREE,
    )(*[far(x) for x in (exponent, *arrays)])


def moments_kernel(start, size, chunks, *refs):
    inputs, outs, bufs, sems = refs[:3], refs[-8:-6], refs[-6:-1], refs[-1]
    high = size // chunks
    turns = [(pl.ds(start + c * high, high), pl.ds(c * high, high)) for c in range(chunks)]
    fetches = [
        [pltpu.make_async_copy(inputs[a].at[there], bufs[a].at[here], sems.at[c, a]) for a in range(3)]
        for c, (there, here) in enumerate(turns)
    ]
    stores = [
        [pltpu.make_async_copy(bufs[3 + a].at[here], outs[a].at[there], sems.at[c, 3 + a]) for a in range(2)]
        for c, (there, here) in enumerate(turns)
    ]
    for row in fetches:
        for f in row:
            f.start()
    for c, (_, here) in enumerate(turns):
        for f in fetches[c]:
            f.wait()
        bufs[3][here, :], bufs[4][here, :] = step(bufs[0][here, :], bufs[1][here, :], bufs[2][here, :])
        for s in stores[c]:
            s.start()
    for row in stores:
        for s in row:
            s.wait()


def moments(arrays, start, size, made=(), chunks=4):
    rows, full = arrays[0].shape
    chunks = min(chunks, size // 8)
    return pl.pallas_call(
        functools.partial(moments_kernel, start, size, chunks),
        in_specs=[FAR] * (3 + len(made)),
        out_specs=[FAR] * 2,
        out_shape=[like((rows, full), F32)] * 2,
        scratch_shapes=[pltpu.VMEM((size, full), F32)] * 5 + [pltpu.SemaphoreType.DMA((chunks, 5))],
        input_output_aliases={3 + i: i for i in range(len(made))},
        compiler_params=pltpu.CompilerParams(vmem_limit_bytes=16 * MIB),
        cost_estimate=pl.CostEstimate(flops=0, bytes_accessed=60 * rows * full, transcendentals=0),
    )(*[far(x) for x in (*arrays, *made)])


def multiply(piece_refs, labels, weight, plan, out_refs):
    stacked = jnp.concatenate([r[...] for r in piece_refs], axis=0)
    total = jnp.dot(stacked, weight, preferred_element_type=F32)
    tall = total.shape[0] // len(labels)
    for wanted, out_ref in zip(plan, out_refs):
        for n, label in enumerate(wanted):
            at = labels.index(label) * tall
            out_ref[n * tall : (n + 1) * tall, :] = total[at : at + tall].astype(out_ref.dtype)


def joined(tall, cols, plan, types):
    return [like((len(wanted) * tall, cols), t) for wanted, t in zip(plan, types)]


def places(heads, rows):
    core, mine = lax.axis_index("dp") % PAIR, lax.axis_index("tensor")
    for n in range(PAIR * heads):
        yield ((core ^ (n // heads)) * heads + (mine ^ (n % heads))) * rows


def fetch_kernel(heads, stale_far, out_ref, sems):
    blocks, rows = out_ref.shape[:2]
    copies = []
    for n, at in enumerate(places(heads, rows)):
        first = (lax.axis_index("dp") // PAIR) * (blocks * rows) + at
        source = stale_far.at[pl.ds(pl.multiple_of(first, rows), rows), :]
        copies.append(pltpu.make_async_copy(source, out_ref.at[n], sems.at[n]))
        copies[-1].start()
    for copy in copies:
        copy.wait()


def fetch(stale, heads, slabs):
    blocks = PAIR * heads
    return pl.pallas_call(
        functools.partial(fetch_kernel, heads),
        in_specs=[FAR],
        out_specs=NEAR,
        out_shape=like((blocks, stale.shape[0] // slabs // blocks, stale.shape[1]), BF16),
        scratch_shapes=[pltpu.SemaphoreType.DMA((blocks,))],
        compiler_params=pltpu.CompilerParams(vmem_limit_bytes=8 * MIB),
        cost_estimate=FREE,
    )(far(stale))


def merge_kernel(heads, labels, plan, stale_ref, *refs):
    blocks = PAIR * heads
    delta_refs, piece_refs = refs[:blocks], refs[blocks : -(len(plan) + 1)]
    weight_ref, *out_refs = refs[-(len(plan) + 1) :]
    rows = delta_refs[0].shape[0]
    for n, at in enumerate(places(heads, rows)):
        here = pl.ds(pl.multiple_of(at, rows), rows)
        weight_ref[here, :] = (stale_ref[n].astype(F32) + delta_refs[n][...].astype(F32)).astype(BF16)
    multiply(piece_refs, labels, weight_ref[...], plan, out_refs)


def product_kernel(labels, plan, *refs):
    *piece_refs, weight_ref = refs[: -len(plan)]
    multiply(piece_refs, labels, weight_ref[...], plan, refs[-len(plan) :])


def merge_product(stale, deltas, pieces, heads, labels, plan, types):
    rows, cols = deltas[0].shape
    blocks = len(deltas)
    tall = sum(p.shape[0] for p in pieces) // len(labels)
    return pl.pallas_call(
        functools.partial(merge_kernel, heads, labels, plan),
        out_shape=[like((blocks * rows, cols), BF16)] + joined(tall, cols, plan, types),
        compiler_params=pltpu.CompilerParams(vmem_limit_bytes=16 * MIB),
        cost_estimate=pl.CostEstimate(flops=0, bytes_accessed=8 * blocks * rows * cols, transcendentals=0),
    )(*[near_by(x) for x in (stale, *deltas, *pieces)])


def product(pieces, weight, labels, plan, types):
    tall = sum(p.shape[0] for p in pieces) // len(labels)
    return pl.pallas_call(
        functools.partial(product_kernel, labels, plan),
        out_shape=joined(tall, weight.shape[1], plan, types),
        compiler_params=pltpu.CompilerParams(vmem_limit_bytes=12 * MIB),
        cost_estimate=FREE,
    )(*[near_by(x) for x in (*pieces, weight)])


def on_device(tokens, gain, stale, bias, first, second, grad, residual, exponent):
    heads = lax.axis_size("tensor")
    replicas = lax.axis_size("dp")
    slabs = replicas // PAIR
    partners = slabs // PAIR
    near, remote = range(partners // 2), range(partners // 2, partners)
    core, mine = lax.axis_index("dp") % PAIR, lax.axis_index("tensor")
    height = tokens.shape[0]

    def over_tensor(x, j):
        return x if j == 0 else lax.ppermute(x, "tensor", [(i, i ^ j) for i in range(heads)])

    def over_core(x):
        return lax.ppermute(x, "dp", [(i, i ^ 1) for i in range(replicas)])

    def over_slab(x, m):
        pairs = [(i, ((i // PAIR) ^ apart(m, i % PAIR)) * PAIR + i % PAIR) for i in range(replicas)]
        return lax.ppermute(x, "dp", pairs)

    def over_next(x):
        return lax.ppermute(x, "dp", [(i, i ^ PAIR) for i in range(replicas)])

    beside = over_core(tokens)
    arrays = (first, second, grad, residual)
    theirs = delta(arrays, exponent, heads, 1, heads - 1)
    theirs, beside = lax.optimization_barrier((theirs, beside))
    arrived = [over_tensor(theirs[j], j + 1) for j in range(heads - 1)]
    normed = norm(tokens, beside, gain, slabs)
    order = (*remote, *near)
    pieces = [over_slab(normed[m], m) for m in order]
    exponent, normed = lax.optimization_barrier((exponent, normed))
    ours = delta(arrays, exponent, heads, 0, 1)
    distant, close = pieces[: len(remote)], pieces[len(remote) :]

    def over_heads(group):
        return [[over_tensor(x, j) for x in group] for j in range(1, heads)]

    ours, close = lax.optimization_barrier((ours, close))
    moved_close = over_heads(close)
    first_rows = first.shape[0]
    bulk = first_rows * 3 // 4
    made = moments(arrays[:3], 0, bulk)
    held = fetch(stale, heads, slabs)
    made, held, distant, arrived, moved_close = lax.optimization_barrier((made, held, distant, arrived, moved_close))
    moved_distant = over_heads(distant)
    shared = [*ours, *arrived]
    shared = shared + [over_core(x) for x in shared]
    peers = range(1, heads)
    evens, odds = remote[::2], remote[1::2]
    labels = [(0, m) for m in remote]
    plan = [[(0, m)] for m in (*evens, *odds)]
    types = [F32] * len(evens) + [BF16] * len(odds)
    weight, *parts = merge_product(held, shared, distant, heads, labels, plan, types)
    ours_even, ours_odd = parts[: len(evens)], parts[len(evens) :]
    met = [over_next(x) for x in ours_odd]
    labels = [(j, m) for j in range(heads) for m in near]
    plan = [[(j, m) for j in range(heads)] for m in near[::2]]
    plan += [[(j, m) for j in group] for group in ([0], peers) for m in near[1::2]]
    blocks = [*close, *[x for row in moved_close for x in row]]
    parts_near = product(blocks, weight, labels, plan, [BF16] * len(plan))
    split = len(near[::2])
    last = split + len(near[1::2])
    terms_near = [over_slab(x, m) for x, m in zip(parts_near[:split], near[::2])]
    middle, late = parts_near[split:last], parts_near[last:]
    met, moved_distant = lax.optimization_barrier((met, moved_distant))

    labels = [(j, m) for j in peers for m in remote]
    plan = [[(j, m) for j in peers] for m in (*evens, *odds)]
    parts = product([x for row in moved_distant for x in row], weight, labels, plan, types[: len(remote)])
    theirs_even, theirs_odd = parts[: len(evens)], parts[len(evens) :]
    theirs_odd, middle = lax.optimization_barrier((theirs_odd, middle))
    met_theirs = [over_next(x) for x in theirs_odd]

    def onward(even, arrived):
        return [over_slab((x + y.astype(F32)).astype(BF16), m) for x, y, m in zip(even, arrived, evens)]

    terms_ours = [over_slab(x, m) for x, m in zip(middle, near[1::2])]
    terms_ours += onward(ours_even, met)
    met_theirs, late = lax.optimization_barrier((met_theirs, late))
    terms_theirs = onward(theirs_even, met_theirs)
    terms_theirs += [over_slab(x, m) for x, m in zip(late, near[1::2])]
    new_first, new_second = moments(arrays[:3], bulk, first_rows - bulk, made)
    new_first, new_second, terms_near, terms_ours, terms_theirs = lax.optimization_barrier(
        (new_first, new_second, terms_near, terms_ours, terms_theirs)
    )

    def added(terms):
        return sum(x.astype(F32) for x in terms).reshape(-1, PAIR, height, weight.shape[1])

    total = added(terms_near) + jnp.concatenate([added(terms_ours), added(terms_theirs)], axis=0)
    keep = jnp.where(core == 0, total[:, 0], total[:, 1])
    give = jnp.where(core == 0, total[:, 1], total[:, 0])
    results = (keep + over_core(give.astype(BF16)).astype(F32) + bias).astype(BF16)
    if heads == 2:
        ordered = jnp.where(mine == 0, results, results[::-1])
    else:
        ordered = jnp.take(results, jnp.arange(heads) ^ mine, axis=0)
    projected = ordered.reshape(-1, results.shape[-1])
    return (new_first, new_second, projected)


def solution(mesh):
    rows = P(("dp", "tensor"), None)
    return jax.shard_map(
        on_device,
        mesh=mesh,
        in_specs=(rows, P(), P(None, "tensor"), P("tensor"), rows, rows, rows, rows, rows),
        out_specs=(rows, rows, P("dp", "tensor")),
        check_vma=False,
    )
```

```python
import functools

import jax
import jax.numpy as jnp
from jax import lax
from jax.experimental import pallas as pl
from jax.experimental.pallas import tpu as pltpu
from jax.sharding import PartitionSpec as P

PAIR = 2
CLIP = 448.0
MIB = 1024 * 1024
F32 = jnp.float32
BF16 = jnp.bfloat16
FAR = pl.BlockSpec(memory_space=pltpu.HBM)
NEAR = pl.BlockSpec(memory_space=pltpu.VMEM)
FREE = pl.CostEstimate(flops=0, bytes_accessed=0, transcendentals=0)


def far(x):
    return pltpu.with_memory_space_constraint(x, pltpu.HBM)


def near_by(x):
    return pltpu.with_memory_space_constraint(x, pltpu.VMEM)


def like(shape, dtype):
    return jax.ShapeDtypeStruct(shape, dtype)


def apart(m, core):
    return (m // 2) * 4 + core * 2 + m % 2


def norm_kernel(ours_ref, theirs_ref, gain_ref, *piece_refs):
    dp = lax.axis_index("dp")
    slab, core = dp // PAIR, dp % PAIR
    height = ours_ref.shape[0]
    width = piece_refs[0].shape[1]
    for turn, ref in enumerate((ours_ref, theirs_ref)):
        values = ref[...].astype(F32)
        scale = lax.rsqrt(jnp.mean(values * values, axis=1, keepdims=True) + 1e-06)
        rows = pl.ds(pl.multiple_of((core ^ turn) * height, height), height)
        for m, piece_ref in enumerate(piece_refs):
            columns = pl.ds(pl.multiple_of((slab ^ apart(m, core)) * width, width), width)
            piece_ref[rows, :] = (ref[:, columns].astype(F32) * scale * gain_ref[:, columns]).astype(BF16)


def norm(ours, theirs, gain, slabs):
    height, features = ours.shape
    return pl.pallas_call(
        norm_kernel,
        out_shape=[like((PAIR * height, features // slabs), BF16)] * (slabs // PAIR),
        compiler_params=pltpu.CompilerParams(vmem_limit_bytes=8 * MIB),
        cost_estimate=FREE,
    )(*[near_by(x) for x in (ours, theirs, gain.reshape(1, features))])


def step(first, second, grad):
    return 0.9 * first + 0.1 * grad, 0.95 * second + 0.05 * grad * grad


def delta_kernel(chunks, qrows, qcol, heads, start, count, *refs):
    expo_far, *inputs = refs[:5]
    delta_outs, (b0, b1, b2, b3, expo_ref, sems, expo_sem) = refs[5 : 5 + count], refs[5 + count :]
    bufs = (b0, b1, b2, b3)
    mine = lax.axis_index("tensor")
    rows = inputs[0].shape[0]
    cols = inputs[0].shape[1] // heads
    groups = cols // qcol
    high = rows // chunks
    fetch_expo = pltpu.make_async_copy(expo_far, expo_ref, expo_sem)
    fetch_expo.start()
    turns = [(j, c) for j in range(count) for c in range(chunks)]
    fetches = []
    for n, (j, c) in enumerate(turns):
        here = (j, pl.ds(c * high, high), slice(None))
        at = pl.ds(c * high, high), pl.ds(pl.multiple_of((mine ^ (start + j)) * cols, cols), cols)
        fetches.append([pltpu.make_async_copy(inputs[a].at[at], bufs[a].at[here], sems.at[n, a]) for a in range(4)])
        for f in fetches[-1]:
            f.start()
    fetch_expo.wait()
    for n, (j, c) in enumerate(turns):
        for f in fetches[n]:
            f.wait()
        for b in range(high // qrows):
            row = c * (high // qrows) + b
            here = pl.ds(row * qrows, qrows)
            for g in range(groups):
                lanes = pl.ds(g * qcol, qcol)
                new_first, new_second = step(b0[j, here, lanes], b1[j, here, lanes], b2[j, here, lanes])
                corrected = 0.02 * new_first / (jnp.sqrt(new_second) + 1e-08) + b3[j, here, lanes]
                expo = jnp.full((1, qcol), expo_ref[row, (mine ^ (start + j)) * groups + g], jnp.int32).astype(F32)
                most = CLIP * jnp.exp2(-expo)
                delta_outs[j][here, lanes] = jnp.clip(corrected, -most, most).astype(BF16)


def delta(arrays, exponent, heads, start, count, chunks=8):
    rows, full = arrays[0].shape
    qrows, qcol = rows // exponent.shape[0], full // exponent.shape[1]
    cols = full // heads
    chunks = min(chunks, rows // qrows)
    return pl.pallas_call(
        functools.partial(delta_kernel, chunks, qrows, qcol, heads, start, count),
        in_specs=[FAR] * 5,
        out_specs=[NEAR] * count,
        out_shape=[like((rows, cols), BF16)] * count,
        scratch_shapes=[pltpu.VMEM((count, rows, cols), F32)] * 4
        + [
            pltpu.SMEM(exponent.shape, jnp.int32),
            pltpu.SemaphoreType.DMA((count * chunks, 4)),
            pltpu.SemaphoreType.DMA(()),
        ],
        compiler_params=pltpu.CompilerParams(vmem_limit_bytes=16 * MIB),
        cost_estimate=FREE,
    )(*[far(x) for x in (exponent, *arrays)])


def moments_kernel(start, size, chunks, *refs):
    inputs, outs, bufs, sems = refs[:3], refs[-8:-6], refs[-6:-1], refs[-1]
    high = size // chunks
    turns = [(pl.ds(start + c * high, high), pl.ds(c * high, high)) for c in range(chunks)]
    fetches = [
        [pltpu.make_async_copy(inputs[a].at[there], bufs[a].at[here], sems.at[c, a]) for a in range(3)]
        for c, (there, here) in enumerate(turns)
    ]
    stores = [
        [pltpu.make_async_copy(bufs[3 + a].at[here], outs[a].at[there], sems.at[c, 3 + a]) for a in range(2)]
        for c, (there, here) in enumerate(turns)
    ]
    for row in fetches:
        for f in row:
            f.start()
    for c, (_, here) in enumerate(turns):
        for f in fetches[c]:
            f.wait()
        bufs[3][here, :], bufs[4][here, :] = step(bufs[0][here, :], bufs[1][here, :], bufs[2][here, :])
        for s in stores[c]:
            s.start()
    for row in stores:
        for s in row:
            s.wait()


def moments(arrays, start, size, made=(), chunks=4):
    rows, full = arrays[0].shape
    chunks = min(chunks, size // 8)
    return pl.pallas_call(
        functools.partial(moments_kernel, start, size, chunks),
        in_specs=[FAR] * (3 + len(made)),
        out_specs=[FAR] * 2,
        out_shape=[like((rows, full), F32)] * 2,
        scratch_shapes=[pltpu.VMEM((size, full), F32)] * 5 + [pltpu.SemaphoreType.DMA((chunks, 5))],
        input_output_aliases={3 + i: i for i in range(len(made))},
        compiler_params=pltpu.CompilerParams(vmem_limit_bytes=16 * MIB),
        cost_estimate=pl.CostEstimate(flops=0, bytes_accessed=60 * rows * full, transcendentals=0),
    )(*[far(x) for x in (*arrays, *made)])


def multiply(piece_refs, labels, weight, plan, out_refs):
    stacked = jnp.concatenate([r[...] for r in piece_refs], axis=0)
    total = jnp.dot(stacked, weight, preferred_element_type=F32)
    tall = total.shape[0] // len(labels)
    for wanted, out_ref in zip(plan, out_refs):
        for n, label in enumerate(wanted):
            at = labels.index(label) * tall
            out_ref[n * tall : (n + 1) * tall, :] = total[at : at + tall].astype(out_ref.dtype)


def joined(tall, cols, plan, types):
    return [like((len(wanted) * tall, cols), t) for wanted, t in zip(plan, types)]


def places(heads, rows):
    core, mine = lax.axis_index("dp") % PAIR, lax.axis_index("tensor")
    for n in range(PAIR * heads):
        yield ((core ^ (n // heads)) * heads + (mine ^ (n % heads))) * rows


def fetch_kernel(heads, stale_far, out_ref, sems):
    blocks, rows = out_ref.shape[:2]
    copies = []
    for n, at in enumerate(places(heads, rows)):
        first = (lax.axis_index("dp") // PAIR) * (blocks * rows) + at
        source = stale_far.at[pl.ds(pl.multiple_of(first, rows), rows), :]
        copies.append(pltpu.make_async_copy(source, out_ref.at[n], sems.at[n]))
        copies[-1].start()
    for copy in copies:
        copy.wait()


def fetch(stale, heads, slabs):
    blocks = PAIR * heads
    return pl.pallas_call(
        functools.partial(fetch_kernel, heads),
        in_specs=[FAR],
        out_specs=NEAR,
        out_shape=like((blocks, stale.shape[0] // slabs // blocks, stale.shape[1]), BF16),
        scratch_shapes=[pltpu.SemaphoreType.DMA((blocks,))],
        compiler_params=pltpu.CompilerParams(vmem_limit_bytes=8 * MIB),
        cost_estimate=FREE,
    )(far(stale))


def merge_kernel(heads, labels, plan, stale_ref, *refs):
    blocks = PAIR * heads
    delta_refs, piece_refs = refs[:blocks], refs[blocks : -(len(plan) + 1)]
    weight_ref, *out_refs = refs[-(len(plan) + 1) :]
    rows = delta_refs[0].shape[0]
    for n, at in enumerate(places(heads, rows)):
        here = pl.ds(pl.multiple_of(at, rows), rows)
        weight_ref[here, :] = (stale_ref[n].astype(F32) + delta_refs[n][...].astype(F32)).astype(BF16)
    multiply(piece_refs, labels, weight_ref[...], plan, out_refs)


def product_kernel(labels, plan, *refs):
    *piece_refs, weight_ref = refs[: -len(plan)]
    multiply(piece_refs, labels, weight_ref[...], plan, refs[-len(plan) :])


def merge_product(stale, deltas, pieces, heads, labels, plan, types):
    rows, cols = deltas[0].shape
    blocks = len(deltas)
    tall = sum(p.shape[0] for p in pieces) // len(labels)
    return pl.pallas_call(
        functools.partial(merge_kernel, heads, labels, plan),
        out_shape=[like((blocks * rows, cols), BF16)] + joined(tall, cols, plan, types),
        compiler_params=pltpu.CompilerParams(vmem_limit_bytes=16 * MIB),
        cost_estimate=pl.CostEstimate(flops=0, bytes_accessed=8 * blocks * rows * cols, transcendentals=0),
    )(*[near_by(x) for x in (stale, *deltas, *pieces)])


def product(pieces, weight, labels, plan, types):
    tall = sum(p.shape[0] for p in pieces) // len(labels)
    return pl.pallas_call(
        functools.partial(product_kernel, labels, plan),
        out_shape=joined(tall, weight.shape[1], plan, types),
        compiler_params=pltpu.CompilerParams(vmem_limit_bytes=12 * MIB),
        cost_estimate=FREE,
    )(*[near_by(x) for x in (*pieces, weight)])


def on_device(tokens, gain, stale, bias, first, second, grad, residual, exponent):
    heads = lax.axis_size("tensor")
    replicas = lax.axis_size("dp")
    slabs = replicas // PAIR
    partners = slabs // PAIR
    near, remote = range(partners // 2), range(partners // 2, partners)
    core, mine = lax.axis_index("dp") % PAIR, lax.axis_index("tensor")
    height = tokens.shape[0]

    def over_tensor(x, j):
        return x if j == 0 else lax.ppermute(x, "tensor", [(i, i ^ j) for i in range(heads)])

    def over_core(x):
        return lax.ppermute(x, "dp", [(i, i ^ 1) for i in range(replicas)])

    def over_slab(x, m):
        pairs = [(i, ((i // PAIR) ^ apart(m, i % PAIR)) * PAIR + i % PAIR) for i in range(replicas)]
        return lax.ppermute(x, "dp", pairs)

    def over_next(x):
        return lax.ppermute(x, "dp", [(i, i ^ PAIR) for i in range(replicas)])

    beside = over_core(tokens)
    arrays = (first, second, grad, residual)
    theirs = delta(arrays, exponent, heads, 1, heads - 1)
    theirs, beside = lax.optimization_barrier((theirs, beside))
    arrived = [over_tensor(theirs[j], j + 1) for j in range(heads - 1)]
    normed = norm(tokens, beside, gain, slabs)
    order = (*remote, *near)
    pieces = [over_slab(normed[m], m) for m in order]
    exponent, normed = lax.optimization_barrier((exponent, normed))
    ours = delta(arrays, exponent, heads, 0, 1)
    distant, close = pieces[: len(remote)], pieces[len(remote) :]

    def over_heads(group):
        return [[over_tensor(x, j) for x in group] for j in range(1, heads)]

    ours, close = lax.optimization_barrier((ours, close))
    moved_close = over_heads(close)
    first_rows = first.shape[0]
    bulk = first_rows * 3 // 4
    made = moments(arrays[:3], 0, bulk)
    held = fetch(stale, heads, slabs)
    made, held, distant, arrived, moved_close = lax.optimization_barrier((made, held, distant, arrived, moved_close))
    moved_distant = over_heads(distant)
    shared = [*ours, *arrived]
    shared = shared + [over_core(x) for x in shared]
    peers = range(1, heads)
    evens, odds = remote[::2], remote[1::2]
    labels = [(0, m) for m in remote]
    plan = [[(0, m)] for m in (*evens, *odds)]
    types = [F32] * len(evens) + [BF16] * len(odds)
    weight, *parts = merge_product(held, shared, distant, heads, labels, plan, types)
    ours_even, ours_odd = parts[: len(evens)], parts[len(evens) :]
    met = [over_next(x) for x in ours_odd]
    labels = [(j, m) for j in range(heads) for m in near]
    plan = [[(j, m) for j in range(heads)] for m in near[::2]]
    plan += [[(j, m) for j in group] for group in ([0], peers) for m in near[1::2]]
    blocks = [*close, *[x for row in moved_close for x in row]]
    parts_near = product(blocks, weight, labels, plan, [BF16] * len(plan))
    split = len(near[::2])
    last = split + len(near[1::2])
    terms_near = [over_slab(x, m) for x, m in zip(parts_near[:split], near[::2])]
    middle, late = parts_near[split:last], parts_near[last:]
    met, moved_distant = lax.optimization_barrier((met, moved_distant))

    labels = [(j, m) for j in peers for m in remote]
    plan = [[(j, m) for j in peers] for m in (*evens, *odds)]
    parts = product([x for row in moved_distant for x in row], weight, labels, plan, types[: len(remote)])
    theirs_even, theirs_odd = parts[: len(evens)], parts[len(evens) :]
    theirs_odd, middle = lax.optimization_barrier((theirs_odd, middle))
    met_theirs = [over_next(x) for x in theirs_odd]

    def onward(even, arrived):
        return [over_slab((x + y.astype(F32)).astype(BF16), m) for x, y, m in zip(even, arrived, evens)]

    terms_ours = [over_slab(x, m) for x, m in zip(middle, near[1::2])]
    terms_ours += onward(ours_even, met)
    met_theirs, late = lax.optimization_barrier((met_theirs, late))
    terms_theirs = onward(theirs_even, met_theirs)
    terms_theirs += [over_slab(x, m) for x, m in zip(late, near[1::2])]
    new_first, new_second = moments(arrays[:3], bulk, first_rows - bulk, made)
    new_first, new_second, terms_near, terms_ours, terms_theirs = lax.optimization_barrier(
        (new_first, new_second, terms_near, terms_ours, terms_theirs)
    )

    def added(terms):
        return sum(x.astype(F32) for x in terms).reshape(-1, PAIR, height, weight.shape[1])

    total = added(terms_near) + jnp.concatenate([added(terms_ours), added(terms_theirs)], axis=0)
    keep = jnp.where(core == 0, total[:, 0], total[:, 1])
    give = jnp.where(core == 0, total[:, 1], total[:, 0])
    results = (keep + over_core(give.astype(BF16)).astype(F32) + bias).astype(BF16)
    if heads == 2:
        ordered = jnp.where(mine == 0, results, results[::-1])
    else:
        ordered = jnp.take(results, jnp.arange(heads) ^ mine, axis=0)
    projected = ordered.reshape(-1, results.shape[-1])
    return (new_first, new_second, projected)


def solution(mesh):
    rows = P(("dp", "tensor"), None)
    return jax.shard_map(
        on_device,
        mesh=mesh,
        in_specs=(rows, P(), P(None, "tensor"), P("tensor"), rows, rows, rows, rows, rows),
        out_specs=(rows, rows, P("dp", "tensor")),
        check_vma=False,
    )
```
